32 devices in a mesh: section: 2 (over x), dp: 4 (over z), tensor: 4 (over y, core).
Axes of the slice: x: 2, y: 2, z: 4, core: 2. Of those that a mesh axis runs over, the one named last changes fastest.
Arguments:
- queries: bfloat16 [2, 1024, 8192], P('section', 'dp', 'tensor'), may hold values from -256 to 256
- image: bfloat16 [8192, 512], P(('section', 'tensor'), 'dp'), may hold values from -6 to 6
- w_key: bfloat16 [2, 8192, 1024], P('section', None, 'tensor'), may hold values from -0.0625 to 0.0625
- w_value: bfloat16 [2, 8192, 1024], P('section', None, 'tensor'), may hold values from -0.0625 to 0.0625
- gates: float32 [2], P('section'), may hold values from 0.3 to 1.5
- tiles: int32 [4], P('dp'), may hold values from 1 to 4, as said below
- cotangent: bfloat16 [2, 1024, 8192], P('section', 'dp', 'tensor'), may hold values from -6 to 6
Outputs:
- attended: bfloat16 [2, 1024, 8192], P('section', 'dp', 'tensor')
- d_queries: bfloat16 [2, 1024, 8192], P('section', 'dp', 'tensor')
- d_image: bfloat16 [8192, 512], P(('section', 'tensor'), 'dp')
The draws below stay inside these ranges and needn't reach their ends.
Inputs may be any that keep to these rules, and one draw needn't show every extreme that they name: The first tiles[b] * 32 image tokens are valid for sample b; some sample has 4 tiles and some has one.
All inputs are finite; a program needn't handle non-finite values.
Results may differ from the reference program's by a relative error of at most 0.013.
The reference program's roundings to bfloat16 on the way (of `key_rows`, `value_rows`, `probs_b`, `d_context`, `d_values`, `d_scores` and `d_keys`) count: a program that leaves them out, or rounds other values in their place, can miss the bound.
Values may be sent and summed in bfloat16 or wider, within the bound.
A program may use at most 64 MiB of HBM per device.

```python
import math
import jax
import jax.numpy as jnp
from jax import lax

D = 8192
HEADS = 64
KV_HEADS = 8
HD = 128
TILES_MAX = 4
TILE_TOK = 32
TXT = 256
IMG = 128
N_SECTION = 2
N_DP = 4


def draw_tiles(key, part):
    first, second, third = jax.random.split(jax.random.fold_in(key, 11), 3)
    counts = jax.random.randint(first, (N_DP,), 1, TILES_MAX + 1)
    spot_high = jax.random.randint(second, (), 0, N_DP)
    spot_low = (spot_high + 1 + jax.random.randint(third, (), 0, N_DP - 1)) % N_DP
    places = jnp.arange(N_DP)
    counts = jnp.where(places == spot_low, 1, counts)
    counts = jnp.where(places == spot_high, TILES_MAX, counts)
    return counts.astype(jnp.int32)


def draw_queries(key, part):
    first = jax.random.fold_in(jax.random.fold_in(key, 23), 0)
    shape = (N_SECTION, N_DP * TXT, HEADS * HD)
    values = jnp.clip(jax.random.normal(first, shape, jnp.float32), -6.0, 6.0)
    return values.astype(jnp.bfloat16)


def level_of(key, shape, cuts, least, top_value):
    gain, own = 1.0, jax.random.fold_in(key, 6)
    for position, parts in cuts:
        heights = jnp.exp(jax.random.uniform(jax.random.fold_in(own, position), (parts,), jnp.float32, least / len(cuts), top_value / len(cuts)))
        gain = gain * jnp.repeat(heights, shape[position] // parts).reshape([-1 if axis == position else 1 for axis in range(len(shape))])
    return gain


def noise(rng, shape, deviation, bound, shards=(), held_as=jnp.bfloat16):
    array = jax.random.normal(rng, shape, jnp.float32) * deviation
    if len(shards) > 0:
        array = level_of(rng, shape, shards, -0.22, 0.18) * array
    return jnp.clip(array, min=-bound, max=bound).astype(held_as)


def setup_inputs(seed: int = 0) -> dict:
    key_list = jax.random.split(jax.random.key(seed), 8)
    return {
        "queries": draw_queries(jax.random.fold_in(key_list[7], 71), 0),
        "image": noise(key_list[1], (D, N_DP * IMG), 1.0, 6.0, ((0, 8), (1, 4))),
        "w_key": noise(key_list[2], (N_SECTION, D, KV_HEADS * HD), D ** -0.5, 0.0625, ((0, 2), (2, 4))),
        "w_value": noise(key_list[3], (N_SECTION, D, KV_HEADS * HD), D ** -0.5, 0.0625, ((0, 2), (2, 4))),
        "gates": jnp.clip(0.3 + 1.2 * jax.random.uniform(key_list[4], (N_SECTION,), jnp.float32) ** level_of(key_list[4], (N_SECTION,), ((0, 2),), -0.2, 0.2), 0.3, 1.5),
        "tiles": draw_tiles(jax.random.fold_in(key_list[7], 71), 0),
        "cotangent": noise(key_list[6], (N_SECTION, N_DP * TXT, HEADS * HD), 1.0, 6.0, ((0, 2), (1, 4), (2, 4))),
    }


def one_sample(text, features, weight_key, weight_value, gate_value, valid_count, upstream):
    tokens = text.shape[0]
    img_count = features.shape[1]
    width = weight_key.shape[1]
    kv_count = width // HD
    q_count = text.shape[1] // HD
    group = q_count // kv_count
    key_rows = jnp.dot(features.T, weight_key, preferred_element_type=jnp.float32).astype(jnp.bfloat16)
    value_rows = jnp.dot(features.T, weight_value, preferred_element_type=jnp.float32).astype(jnp.bfloat16)
    query_heads = text.astype(jnp.float32).reshape(tokens, kv_count, group, HD)
    key_heads = key_rows.astype(jnp.float32).reshape(img_count, kv_count, HD)
    value_heads = value_rows.astype(jnp.float32).reshape(img_count, kv_count, HD)
    scores = jnp.einsum('tkgd,skd->kgts', query_heads, key_heads) / math.sqrt(HD)
    allowed = jnp.arange(img_count) < valid_count
    scores = jnp.where(allowed, scores, jnp.float32(-1e+30))
    top = lax.optimization_barrier(jnp.max(scores, axis=-1, keepdims=True))
    expo = jnp.exp(scores - top)
    probs = expo / lax.optimization_barrier(jnp.sum(expo, axis=-1, keepdims=True))
    probs_b = probs.astype(jnp.bfloat16).astype(jnp.float32)
    context = jnp.einsum('kgts,skd->tkgd', probs_b, value_heads)
    scale = jnp.tanh(gate_value)
    attended = (scale * context).reshape(tokens, q_count * HD).astype(jnp.bfloat16)
    d_context = (scale * upstream.astype(jnp.float32)).astype(jnp.bfloat16).astype(jnp.float32)
    d_context = d_context.reshape(tokens, kv_count, group, HD)
    d_values = jnp.einsum('kgts,tkgd->skd', probs_b, d_context).astype(jnp.bfloat16)
    d_probs = jnp.einsum('tkgd,skd->kgts', d_context, value_heads)
    delta = lax.optimization_barrier(jnp.sum(probs * d_probs, axis=-1, keepdims=True))
    d_scores = (probs * (d_probs - delta) / math.sqrt(HD)).astype(jnp.bfloat16).astype(jnp.float32)
    d_query = jnp.einsum('kgts,skd->tkgd', d_scores, key_heads).reshape(tokens, q_count * HD).astype(jnp.bfloat16)
    d_keys = jnp.einsum('kgts,tkgd->skd', d_scores, query_heads).astype(jnp.bfloat16)
    d_keys = d_keys.reshape(img_count, width)
    d_values = d_values.reshape(img_count, width)
    term = jnp.dot(weight_key, d_keys.T, preferred_element_type=jnp.float32)
    term = term + jnp.dot(weight_value, d_values.T, preferred_element_type=jnp.float32)
    return (attended, d_query, term)

def reference(queries, image, w_key, w_value, gates, tiles, cotangent):
    n_section = queries.shape[0]
    n_samples = tiles.shape[0]
    width_all = queries.shape[2]
    features = image.reshape(D, n_samples, IMG).transpose(1, 0, 2)
    valid = (tiles * TILE_TOK).astype(jnp.int32)
    attended_all = []
    d_query_all = []
    grad_total = jnp.zeros((n_samples, D, IMG), jnp.float32)
    for section in range(n_section):
        text = queries[section].reshape(n_samples, TXT, width_all)
        upstream = cotangent[section].reshape(n_samples, TXT, width_all)
        runner = jax.vmap(one_sample, in_axes=(0, 0, None, None, None, 0, 0))
        attended, d_query, term = runner(text, features, w_key[section], w_value[section], gates[section], valid, upstream)
        attended_all.append(attended.reshape(n_samples * TXT, width_all))
        d_query_all.append(d_query.reshape(n_samples * TXT, width_all))
        grad_total = grad_total + term
    d_image = grad_total.transpose(1, 0, 2).reshape(D, n_samples * IMG).astype(jnp.bfloat16)
    return (jnp.stack(attended_all), jnp.stack(d_query_all), d_image)
```

```python
import functools
import math

import jax
import jax.numpy as jnp
from jax import lax
from jax.experimental import pallas as pl
from jax.experimental.pallas import tpu as pltpu
from jax.sharding import PartitionSpec as P

HD = 128
TILE_TOK = 32
CORES = 2
MESH = pl.DeviceIdType.MESH
F32 = jnp.float32
BF16 = jnp.bfloat16
NT = (((1,), (1,)), ((), ()))
TN = (((0,), (0,)), ((), ()))
NN = (((1,), (0,)), ((), ()))


def dot(a, b, dims):
    return lax.dot_general(a, b, dims, preferred_element_type=F32)


def counts(n_s, n_y):
    near = (n_s - 1) + (n_y - 1)
    far = (n_s - 1) * (n_y - 1)
    chips = n_s * n_y
    gather_sends = 2 * near + 2 * far + 2 * chips
    scatter_sends = chips + 2 * far + 2 * near
    return gather_sends + scatter_sends


def kernel(
    n_s, n_y, block,
    gates_ref, tiles_ref, q_hbm, img_hbm, wk_hbm, wv_hbm, cot_hbm,
    att_hbm, dq_hbm, dimg_ref,
    wk, wv, q, cot, att, dq, img, acc, kv, dk, dv, dkv_t, probs_t, ds_t,
    pair_out, pair_in, held, out_send, mid, last,
    local_sem, send_sem, img_sem, pair_sem, mid_sem, last_sem,
):
    s = lax.axis_index("section")
    t = lax.axis_index("tensor")
    y = t // CORES
    c = t % CORES
    n_t = n_y * CORES
    chunk = img_hbm.shape[0]
    half = chunk // 2
    slots = img_hbm.shape[1]
    width = wk.shape[1]
    tokens, columns = q.shape
    heads = columns // HD
    group = columns // width
    far = [(ds, dy) for ds in range(1, n_s) for dy in range(1, n_y)]
    near_s = [(ds, 0) for ds in range(1, n_s)]
    near_y = [(0, dy) for dy in range(1, n_y)]

    def place(ds, dy):
        return ds * n_y + dy

    def to(ds, dy, other=False):
        core = 1 - c if other else c
        return {
            "section": lax.rem(s + ds, n_s),
            "tensor": lax.rem(y + dy, n_y) * CORES + core,
        }

    def rows_of(ds, dy, core):
        chip = lax.rem(s + ds + n_s, n_s) * n_t + lax.rem(y + dy + n_y, n_y) * CORES
        return pl.ds(pl.multiple_of((chip + core) * chunk, chunk), chunk)

    sent = []

    def send(src, dst, sem, device):
        copy = pltpu.make_async_remote_copy(
            src_ref=src, dst_ref=dst, send_sem=send_sem.at[len(sent)],
            recv_sem=sem, device_id=device, device_id_type=MESH,
        )
        copy.start()
        sent.append(copy)

    def arrive(dst, sem):
        pltpu.make_async_remote_copy(
            src_ref=dst, dst_ref=dst, send_sem=send_sem.at[0],
            recv_sem=sem, device_id=to(0, 0, True), device_id_type=MESH,
        ).wait_recv()

    local = []

    def bring(src, dst):
        copy = pltpu.make_async_copy(src, dst, local_sem.at[len(local)])
        copy.start()
        local.append(copy)
        return copy

    barrier = pltpu.get_barrier_semaphore()
    partners = [to(0, 0, True)] + [to(ds, dy) for ds, dy in near_s + near_y]
    for device in partners:
        pl.semaphore_signal(barrier, inc=1, device_id=device, device_id_type=MESH)
    own = bring(img_hbm, img.at[0, 0])
    parts = 4
    depth = wk.shape[0] // parts
    weights = []
    for i in range(parts):
        piece = pl.ds(i * depth, depth)
        weights.append(bring(wk_hbm.at[piece], wk.at[piece]))
        weights.append(bring(wv_hbm.at[piece], wv.at[piece]))
    text = [bring(q_hbm, q), bring(cot_hbm, cot)]
    pl.semaphore_wait(barrier, len(partners))

    def piece_of(ds, dy, core, h):
        return img.at[place(ds, dy), core, pl.ds(h * half, half)]

    def own_piece(h):
        return img_hbm.at[pl.ds(h * half, half)]

    for h in range(2):
        for ds, dy in near_s:
            send(own_piece(h), piece_of(ds, dy, 0, h), img_sem.at[place(ds, dy), 0, h], to(ds, dy))
        for ds, dy in near_y:
            send(own_piece(1 - h), piece_of(ds, dy, 0, 1 - h), img_sem.at[place(ds, dy), 0, 1 - h], to(ds, dy))
    for h in range(2):
        send(own_piece(h), piece_of(0, 0, 1, h), img_sem.at[0, 1, h], to(0, 0, True))

    def receive(ds, dy, core, h):
        arrive(piece_of(ds, dy, core, h), img_sem.at[place(ds, dy), core, h])

    def share(ds, dy, h):
        send(piece_of(ds, dy, 0, h), piece_of(ds, dy, 1, h), img_sem.at[place(ds, dy), 1, h], to(0, 0, True))

    def project(ds, dy, core):
        rows = rows_of(-ds, -dy, 1 - c if core else c)
        features = img[place(ds, dy), core]
        acc[:, :width] += dot(features, wk[rows, :], TN)
        acc[:, width:] += dot(features, wv[rows, :], TN)

    for ds, dy in near_s:
        receive(ds, dy, 0, 0)
        for _, ey in near_y:
            send(piece_of(ds, 0, 0, 0), piece_of(ds, ey, 0, 0), img_sem.at[place(ds, ey), 0, 0], to(0, ey))
        share(ds, dy, 0)
    for ds, dy in near_y:
        receive(ds, dy, 0, 1)
        for es, _ in near_s:
            send(piece_of(0, dy, 0, 1), piece_of(es, dy, 0, 1), img_sem.at[place(es, dy), 0, 1], to(es, 0))
        share(ds, dy, 1)
    acc[...] = jnp.zeros_like(acc)
    for copy in weights:
        copy.wait()
    own.wait()
    project(0, 0, 0)
    for h in range(2):
        receive(0, 0, 1, h)
    project(0, 0, 1)
    for ds, dy in near_s:
        receive(ds, dy, 0, 1)
        share(ds, dy, 1)
    for ds, dy in near_y:
        receive(ds, dy, 0, 0)
        share(ds, dy, 0)
    for ds, dy in near_s + near_y:
        project(ds, dy, 0)
    for ds, dy in near_s + near_y:
        for h in range(2):
            receive(ds, dy, 1, h)
        project(ds, dy, 1)
    for ds, dy in far:
        for h in range(2):
            receive(ds, dy, 0, h)
            share(ds, dy, h)
        project(ds, dy, 0)
    for ds, dy in far:
        for h in range(2):
            receive(ds, dy, 1, h)
        project(ds, dy, 1)

    kv[...] = acc[...].astype(BF16)
    dk[...] = jnp.zeros_like(dk)
    dv[...] = jnp.zeros_like(dv)
    for copy in text:
        copy.wait()
    scale = jnp.tanh(jnp.full((1, HD), gates_ref[0], F32))
    valid = tiles_ref[0] * TILE_TOK
    factor = 1.0 / math.sqrt(HD)

    def lanes(i, offset=0):
        return pl.ds(pl.multiple_of(i * HD + offset, HD), HD)

    def attend(b, carry):
        first = b * block
        j = first // group
        key = kv[:, lanes(j)]
        value = kv[:, lanes(j, width)]
        allowed = lax.broadcasted_iota(jnp.int32, (slots, tokens), 0) < valid
        total_k = dk[:, lanes(j)]
        total_v = dv[:, lanes(j)]
        for i in range(block):
            query = q[:, lanes(first + i)]
            upstream = (scale * cot[:, lanes(first + i)].astype(F32)).astype(BF16)
            scores = jnp.where(allowed, dot(key, query, NT) * factor, -1e30)
            expo = jnp.exp(scores - jnp.max(scores, axis=0, keepdims=True))
            probs = expo * (1.0 / jnp.sum(expo, axis=0, keepdims=True))
            probs_b = probs.astype(BF16)
            d_probs = dot(value, upstream, NT)
            delta = jnp.sum(probs * d_probs, axis=0, keepdims=True)
            d_scores = (probs * (d_probs - delta) * factor).astype(BF16)
            total_v += dot(probs_b, upstream, NN)
            total_k += dot(d_scores, query, NN)
            probs_t[first + i] = probs_b
            ds_t[first + i] = d_scores
        dk[:, lanes(j)] = total_k
        dv[:, lanes(j)] = total_v
        return carry

    lax.fori_loop(0, heads // block, attend, 0)
    dkv_t[:width, :] = dk[...].astype(BF16).T
    dkv_t[width:, :] = dv[...].astype(BF16).T

    def finish(b, carry):
        first = b * block
        j = first // group
        key = kv[:, lanes(j)]
        value = kv[:, lanes(j, width)]
        for i in range(block):
            context = dot(probs_t[first + i], value, TN)
            att[:, lanes(first + i)] = (scale * context).astype(BF16)
            dq[:, lanes(first + i)] = dot(ds_t[first + i], key, TN).astype(BF16)
        return carry

    def term(ds, dy, core):
        rows = rows_of(ds, dy, core)
        return dot(wk[rows, :], dkv_t[:width, :], NN) + dot(wv[rows, :], dkv_t[width:, :], NN)

    def start_pair(ds, dy):
        k = place(ds, dy)
        pair_out[k] = term(ds, dy, 1 - c).astype(BF16)
        send(pair_out.at[k], pair_in.at[k], pair_sem.at[k], to(0, 0, True))
        held[k] = term(ds, dy, c)

    def end_pair(ds, dy):
        k = place(ds, dy)
        arrive(pair_in.at[k], pair_sem.at[k])
        total = held[k] + pair_in[k].astype(F32)
        if (ds, dy) in far:
            out_send[k] = total.astype(BF16)
            send(out_send.at[k, pl.ds(0, half)], mid.at[0, k], mid_sem.at[0, k], to(ds, 0))
            send(out_send.at[k, pl.ds(half, half)], mid.at[1, k], mid_sem.at[1, k], to(0, dy))
        else:
            held[k] = total
            if (ds, dy) != (0, 0):
                h = 0 if ds else 1
                pass_on(ds, dy, h)

    def pass_on(ds, dy, h):
        k = place(ds, dy)
        piece = pl.ds(h * half, half)
        out_send[k, piece] = held[k, piece].astype(BF16)
        send(out_send.at[k, piece], last.at[k, piece], last_sem.at[k, h], to(ds, dy))

    order = far + near_s + near_y + [(0, 0)]
    for n, target in enumerate(order):
        start_pair(*target)
        if n:
            end_pair(*order[n - 1])
    end_pair(*order[-1])
    for ds, dy in near_s + near_y:
        k = place(ds, dy)
        h = 1 if ds else 0
        piece = pl.ds(h * half, half)
        for es, ey in far:
            if (es == ds) if ds else (ey == dy):
                m = place(es, ey)
                arrive(mid.at[h, m], mid_sem.at[h, m])
                held[k, piece] += mid[h, m].astype(F32)
        pass_on(ds, dy, h)
    lax.fori_loop(0, heads // block, finish, 0)
    bring(att, att_hbm)
    bring(dq, dq_hbm)
    total = held[0]
    for ds, dy in near_s + near_y:
        k = place(ds, dy)
        for h in range(2):
            arrive(last.at[k, pl.ds(h * half, half)], last_sem.at[k, h])
        total += last[k].astype(F32)
    dimg_ref[...] = total.astype(BF16)
    for copy in local[-2:]:
        copy.wait()
    for copy in sent:
        copy.wait_send()


def solution(mesh):
    n_s = mesh.shape["section"]
    n_t = mesh.shape["tensor"]
    n_y = n_t // CORES
    chips = n_s * n_y

    def shards(queries, image, w_key, w_value, gates, tiles, cotangent):
        text, upstream = queries[0], cotangent[0]
        weight_key, weight_value = w_key[0], w_value[0]
        tokens, columns = text.shape
        d, width = weight_key.shape
        chunk, slots = image.shape
        heads = columns // HD
        group = columns // width
        block = math.gcd(group, 4)
        half = chunk // 2
        smem = pl.BlockSpec(memory_space=pltpu.SMEM)
        anywhere = pl.BlockSpec(memory_space=pl.ANY)
        vmem = pl.BlockSpec(memory_space=pltpu.VMEM)
        dma = pltpu.SemaphoreType.DMA
        attended, d_query, d_image = pl.pallas_call(
            functools.partial(kernel, n_s, n_y, block),
            out_shape=(
                jax.ShapeDtypeStruct((tokens, columns), BF16),
                jax.ShapeDtypeStruct((tokens, columns), BF16),
                jax.ShapeDtypeStruct((chunk, slots), BF16),
            ),
            in_specs=[smem, smem] + [anywhere] * 5,
            out_specs=(anywhere, anywhere, vmem),
            scratch_shapes=[
                pltpu.VMEM((d, width), BF16),
                pltpu.VMEM((d, width), BF16),
                pltpu.VMEM((tokens, columns), BF16),
                pltpu.VMEM((tokens, columns), BF16),
                pltpu.VMEM((tokens, columns), BF16),
                pltpu.VMEM((tokens, columns), BF16),
                pltpu.VMEM((chips, CORES, chunk, slots), BF16),
                pltpu.VMEM((slots, 2 * width), F32),
                pltpu.VMEM((slots, 2 * width), BF16),
                pltpu.VMEM((slots, width), F32),
                pltpu.VMEM((slots, width), F32),
                pltpu.VMEM((2 * width, slots), BF16),
                pltpu.VMEM((heads, slots, tokens), BF16),
                pltpu.VMEM((heads, slots, tokens), BF16),
                pltpu.VMEM((chips, chunk, slots), BF16),
                pltpu.VMEM((chips, chunk, slots), BF16),
                pltpu.VMEM((chips, chunk, slots), F32),
                pltpu.VMEM((chips, chunk, slots), BF16),
                pltpu.VMEM((2, chips, half, slots), BF16),
                pltpu.VMEM((chips, chunk, slots), BF16),
                dma((13,)),
                dma((counts(n_s, n_y),)),
                dma((chips, CORES, 2)),
                dma((chips,)),
                dma((2, chips)),
                dma((chips, 2)),
            ],
            compiler_params=pltpu.CompilerParams(
                collective_id=0, has_side_effects=True, vmem_limit_bytes=48 * 1024 * 1024
            ),
            cost_estimate=pl.CostEstimate(
                flops=8 * d * width * slots + 12 * tokens * columns * slots,
                bytes_accessed=4 * d * width + 8 * tokens * columns,
                transcendentals=heads * tokens * slots,
            ),
        )(gates, tiles, text, image, weight_key, weight_value, upstream)
        return attended[None], d_query[None], d_image

    return jax.shard_map(
        shards,
        mesh=mesh,
        in_specs=(
            P("section", "dp", "tensor"),
            P(("section", "tensor"), "dp"),
            P("section", None, "tensor"),
            P("section", None, "tensor"),
            P("section"),
            P("dp"),
            P("section", "dp", "tensor"),
        ),
        out_specs=(
            P("section", "dp", "tensor"),
            P("section", "dp", "tensor"),
            P(("section", "tensor"), "dp"),
        ),
        check_vma=False,
    )
```

```python
import functools
import math

import jax
import jax.numpy as jnp
from jax import lax
from jax.experimental import pallas as pl
from jax.experimental.pallas import tpu as pltpu
from jax.sharding import PartitionSpec as P

HD = 128
TILE_TOK = 32
CORES = 2
MESH = pl.DeviceIdType.MESH
F32 = jnp.float32
BF16 = jnp.bfloat16
NT = (((1,), (1,)), ((), ()))
TN = (((0,), (0,)), ((), ()))
NN = (((1,), (0,)), ((), ()))


def dot(a, b, dims):
    return lax.dot_general(a, b, dims, preferred_element_type=F32)


def counts(n_s, n_y):
    near = (n_s - 1) + (n_y - 1)
    far = (n_s - 1) * (n_y - 1)
    chips = n_s * n_y
    gather_sends = 2 * near + 2 * far + 2 * chips
    scatter_sends = chips + 2 * far + 2 * near
    return gather_sends + scatter_sends


def kernel(
    n_s, n_y, block,
    gates_ref, tiles_ref, q_hbm, img_hbm, wk_hbm, wv_hbm, cot_hbm,
    att, dq, dimg_ref,
    w, q, cot, img, acc, kv, dk, dv, dkv_t, probs_t, ds_t,
    pair_out, pair_in, held, out_send, mid, last,
    local_sem, send_sem, img_sem, pair_sem, mid_sem, last_sem,
):
    s = lax.axis_index("section")
    t = lax.axis_index("tensor")
    y = t // CORES
    c = t % CORES
    n_t = n_y * CORES
    chunk = img_hbm.shape[0]
    half = chunk // 2
    slots = img_hbm.shape[1]
    width = wk_hbm.shape[1]
    tokens, columns = q.shape
    heads = columns // HD
    group = columns // width
    far = [(ds, dy) for ds in range(1, n_s) for dy in range(1, n_y)]
    near_s = [(ds, 0) for ds in range(1, n_s)]
    near_y = [(0, dy) for dy in range(1, n_y)]

    def place(ds, dy):
        return ds * n_y + dy

    def to(ds, dy, other=False):
        core = 1 - c if other else c
        return {
            "section": lax.rem(s + ds, n_s),
            "tensor": lax.rem(y + dy, n_y) * CORES + core,
        }

    def rows_of(ds, dy, core):
        chip = lax.rem(s + ds + n_s, n_s) * n_t + lax.rem(y + dy + n_y, n_y) * CORES
        return pl.ds(pl.multiple_of((chip + core) * chunk, chunk), chunk)

    sent = []

    def send(src, dst, sem, device):
        copy = pltpu.make_async_remote_copy(
            src_ref=src, dst_ref=dst, send_sem=send_sem.at[len(sent)],
            recv_sem=sem, device_id=device, device_id_type=MESH,
        )
        copy.start()
        sent.append(copy)

    def arrive(dst, sem):
        pltpu.make_async_remote_copy(
            src_ref=dst, dst_ref=dst, send_sem=send_sem.at[0],
            recv_sem=sem, device_id=to(0, 0, True), device_id_type=MESH,
        ).wait_recv()

    local = []

    def bring(src, dst):
        copy = pltpu.make_async_copy(src, dst, local_sem.at[len(local)])
        copy.start()
        local.append(copy)
        return copy

    barrier = pltpu.get_barrier_semaphore()
    partners = [to(0, 0, True)] + [to(ds, dy) for ds, dy in near_s + near_y]
    for device in partners:
        pl.semaphore_signal(barrier, inc=1, device_id=device, device_id_type=MESH)
    own = bring(img_hbm, img.at[0, 0])
    parts = 4
    depth = w.shape[0] // parts
    weights = []
    for i in range(parts):
        piece = pl.ds(i * depth, depth)
        weights.append(bring(wk_hbm.at[piece], w.at[piece, pl.ds(0, width)]))
        weights.append(bring(wv_hbm.at[piece], w.at[piece, pl.ds(width, width)]))
    text = [bring(q_hbm, q), bring(cot_hbm, cot)]
    pl.semaphore_wait(barrier, len(partners))

    def piece_of(ds, dy, core, h):
        return img.at[place(ds, dy), core, pl.ds(h * half, half)]

    def own_piece(h):
        return img_hbm.at[pl.ds(h * half, half)]

    for h in range(2):
        for ds, dy in near_s:
            send(own_piece(h), piece_of(ds, dy, 0, h), img_sem.at[place(ds, dy), 0, h], to(ds, dy))
        for ds, dy in near_y:
            send(own_piece(1 - h), piece_of(ds, dy, 0, 1 - h), img_sem.at[place(ds, dy), 0, 1 - h], to(ds, dy))
    for h in range(2):
        send(own_piece(h), piece_of(0, 0, 1, h), img_sem.at[0, 1, h], to(0, 0, True))

    def receive(ds, dy, core, h):
        arrive(piece_of(ds, dy, core, h), img_sem.at[place(ds, dy), core, h])

    def share(ds, dy, h):
        send(piece_of(ds, dy, 0, h), piece_of(ds, dy, 1, h), img_sem.at[place(ds, dy), 1, h], to(0, 0, True))

    def project(ds, dy, core):
        rows = rows_of(-ds, -dy, 1 - c if core else c)
        features = img[place(ds, dy), core]
        acc[...] += dot(features, w[rows, :], TN)

    for ds, dy in near_s:
        receive(ds, dy, 0, 0)
        for _, ey in near_y:
            send(piece_of(ds, 0, 0, 0), piece_of(ds, ey, 0, 0), img_sem.at[place(ds, ey), 0, 0], to(0, ey))
        share(ds, dy, 0)
    for ds, dy in near_y:
        receive(ds, dy, 0, 1)
        for es, _ in near_s:
            send(piece_of(0, dy, 0, 1), piece_of(es, dy, 0, 1), img_sem.at[place(es, dy), 0, 1], to(es, 0))
        share(ds, dy, 1)
    acc[...] = jnp.zeros_like(acc)
    for copy in weights:
        copy.wait()
    own.wait()
    project(0, 0, 0)
    for h in range(2):
        receive(0, 0, 1, h)
    project(0, 0, 1)
    for copy in text:
        copy.wait()
    scale = jnp.tanh(jnp.full((1, HD), gates_ref[0], F32))
    for i in range(heads):
        part = pl.ds(i * HD, HD)
        cot[:, part] = (scale * cot[:, part].astype(F32)).astype(BF16)
    for ds, dy in near_s:
        receive(ds, dy, 0, 1)
        share(ds, dy, 1)
    for ds, dy in near_y:
        receive(ds, dy, 0, 0)
        share(ds, dy, 0)
    for ds, dy in near_s + near_y:
        project(ds, dy, 0)
    for ds, dy in near_s + near_y:
        for h in range(2):
            receive(ds, dy, 1, h)
        project(ds, dy, 1)
    for ds, dy in far:
        for h in range(2):
            receive(ds, dy, 0, h)
            share(ds, dy, h)
        project(ds, dy, 0)
    for ds, dy in far:
        for h in range(2):
            receive(ds, dy, 1, h)
        project(ds, dy, 1)

    kv[...] = acc[...].astype(BF16)
    dk[...] = jnp.zeros_like(dk)
    dv[...] = jnp.zeros_like(dv)
    valid = tiles_ref[0] * TILE_TOK
    factor = 1.0 / math.sqrt(HD)

    def lanes(i, offset=0):
        return pl.ds(pl.multiple_of(i * HD + offset, HD), HD)

    def attend(b, carry):
        first = b * block
        j = first // group
        key = kv[:, lanes(j)]
        value = kv[:, lanes(j, width)]
        allowed = lax.broadcasted_iota(jnp.int32, (slots, tokens), 0) < valid
        total_k = dk[:, lanes(j)]
        total_v = dv[:, lanes(j)]
        for i in range(block):
            query = q[:, lanes(first + i)]
            upstream = cot[:, lanes(first + i)]
            scores = jnp.where(allowed, dot(key, query, NT) * factor, -1e30)
            expo = jnp.exp(scores - jnp.max(scores, axis=0, keepdims=True))
            probs = expo * (1.0 / jnp.sum(expo, axis=0, keepdims=True))
            probs_b = probs.astype(BF16)
            d_probs = dot(value, upstream, NT)
            delta = jnp.sum(probs * d_probs, axis=0, keepdims=True)
            d_scores = (probs * (d_probs - delta) * factor).astype(BF16)
            total_v += dot(probs_b, upstream, NN)
            total_k += dot(d_scores, query, NN)
            probs_t[first + i] = probs_b
            ds_t[first + i] = d_scores
        dk[:, lanes(j)] = total_k
        dv[:, lanes(j)] = total_v
        return carry

    lax.fori_loop(0, heads // block, attend, 0)
    dkv_t[:width, :] = dk[...].astype(BF16).T
    dkv_t[width:, :] = dv[...].astype(BF16).T

    def finish(b, carry):
        first = b * block
        j = first // group
        key = kv[:, lanes(j)]
        value = kv[:, lanes(j, width)]
        for i in range(block):
            context = dot(probs_t[first + i], value, TN)
            att[:, lanes(first + i)] = (scale * context).astype(BF16)
            dq[:, lanes(first + i)] = dot(ds_t[first + i], key, TN).astype(BF16)
        return carry

    def term(ds, dy, core):
        rows = rows_of(ds, dy, core)
        return dot(w[rows, :], dkv_t[...], NN)

    def start_pair(ds, dy):
        k = place(ds, dy)
        pair_out[k] = term(ds, dy, 1 - c).astype(BF16)
        send(pair_out.at[k], pair_in.at[k], pair_sem.at[k], to(0, 0, True))
        held[k] = term(ds, dy, c)

    def end_pair(ds, dy):
        k = place(ds, dy)
        arrive(pair_in.at[k], pair_sem.at[k])
        total = held[k] + pair_in[k].astype(F32)
        if (ds, dy) in far:
            out_send[k] = total.astype(BF16)
            send(out_send.at[k, pl.ds(0, half)], mid.at[0, k], mid_sem.at[0, k], to(ds, 0))
            send(out_send.at[k, pl.ds(half, half)], mid.at[1, k], mid_sem.at[1, k], to(0, dy))
        else:
            held[k] = total
            if (ds, dy) != (0, 0):
                h = 0 if ds else 1
                pass_on(ds, dy, h)

    def pass_on(ds, dy, h):
        k = place(ds, dy)
        piece = pl.ds(h * half, half)
        out_send[k, piece] = held[k, piece].astype(BF16)
        send(out_send.at[k, piece], last.at[k, piece], last_sem.at[k, h], to(ds, dy))

    order = far + near_s + near_y + [(0, 0)]
    for n, target in enumerate(order):
        start_pair(*target)
        if n:
            end_pair(*order[n - 1])
    end_pair(*order[-1])
    blocks = heads // block
    lax.fori_loop(0, blocks // 2, finish, 0)
    for ds, dy in near_s + near_y:
        k = place(ds, dy)
        h = 1 if ds else 0
        piece = pl.ds(h * half, half)
        for es, ey in far:
            if (es == ds) if ds else (ey == dy):
                m = place(es, ey)
                arrive(mid.at[h, m], mid_sem.at[h, m])
                held[k, piece] += mid[h, m].astype(F32)
        pass_on(ds, dy, h)
    lax.fori_loop(blocks // 2, blocks, finish, 0)
    total = held[0]
    for ds, dy in near_s + near_y:
        k = place(ds, dy)
        for h in range(2):
            arrive(last.at[k, pl.ds(h * half, half)], last_sem.at[k, h])
        total += last[k].astype(F32)
    dimg_ref[...] = total.astype(BF16)
    for copy in sent:
        copy.wait_send()


def write_out(count, *refs):
    sem = refs[-1]
    copies = [pltpu.make_async_copy(refs[i], refs[count + i], sem.at[i]) for i in range(count)]
    for copy in copies:
        copy.start()
    for copy in copies:
        copy.wait()


def solution(mesh):
    n_s = mesh.shape["section"]
    n_t = mesh.shape["tensor"]
    n_y = n_t // CORES
    chips = n_s * n_y

    def shards(queries, image, w_key, w_value, gates, tiles, cotangent):
        text, upstream = queries[0], cotangent[0]
        weight_key, weight_value = w_key[0], w_value[0]
        tokens, columns = text.shape
        d, width = weight_key.shape
        chunk, slots = image.shape
        heads = columns // HD
        group = columns // width
        block = math.gcd(group, 4)
        half = chunk // 2
        smem = pl.BlockSpec(memory_space=pltpu.SMEM)
        vmem = pl.BlockSpec(memory_space=pltpu.VMEM)
        hbm = pl.BlockSpec(memory_space=pltpu.HBM)
        dma = pltpu.SemaphoreType.DMA
        results = pl.pallas_call(
            functools.partial(kernel, n_s, n_y, block),
            out_shape=(
                pltpu.VMEM((tokens, columns), BF16),
                pltpu.VMEM((tokens, columns), BF16),
                pltpu.VMEM((chunk, slots), BF16),
            ),
            in_specs=[smem, smem] + [hbm] * 5,
            out_specs=(vmem, vmem, vmem),
            scratch_shapes=[
                pltpu.VMEM((d, 2 * width), BF16),
                pltpu.VMEM((tokens, columns), BF16),
                pltpu.VMEM((tokens, columns), BF16),
                pltpu.VMEM((chips, CORES, chunk, slots), BF16),
                pltpu.VMEM((slots, 2 * width), F32),
                pltpu.VMEM((slots, 2 * width), BF16),
                pltpu.VMEM((slots, width), F32),
                pltpu.VMEM((slots, width), F32),
                pltpu.VMEM((2 * width, slots), BF16),
                pltpu.VMEM((heads, slots, tokens), BF16),
                pltpu.VMEM((heads, slots, tokens), BF16),
                pltpu.VMEM((chips, chunk, slots), BF16),
                pltpu.VMEM((chips, chunk, slots), BF16),
                pltpu.VMEM((chips, chunk, slots), F32),
                pltpu.VMEM((chips, chunk, slots), BF16),
                pltpu.VMEM((2, chips, half, slots), BF16),
                pltpu.VMEM((chips, chunk, slots), BF16),
                dma((11,)),
                dma((counts(n_s, n_y),)),
                dma((chips, CORES, 2)),
                dma((chips,)),
                dma((2, chips)),
                dma((chips, 2)),
            ],
            compiler_params=pltpu.CompilerParams(
                collective_id=0, has_side_effects=True, vmem_limit_bytes=60 * 1024 * 1024
            ),
            cost_estimate=pl.CostEstimate(
                flops=8 * d * width * slots + 12 * tokens * columns * slots,
                bytes_accessed=4 * d * width + 8 * tokens * columns,
                transcendentals=heads * tokens * slots,
            ),
        )(gates, tiles, text, image, weight_key, weight_value, upstream)
        attended, d_query, d_image = pl.pallas_call(
            functools.partial(write_out, len(results)),
            out_shape=tuple(jax.ShapeDtypeStruct(a.shape, a.dtype) for a in results),
            in_specs=[vmem] * len(results),
            out_specs=tuple(hbm for _ in results),
            scratch_shapes=[dma((len(results),))],
        )(*results)
        return attended[None], d_query[None], d_image

    return jax.shard_map(
        shards,
        mesh=mesh,
        in_specs=(
            P("section", "dp", "tensor"),
            P(("section", "tensor"), "dp"),
            P("section", None, "tensor"),
            P("section", None, "tensor"),
            P("section"),
            P("dp"),
            P("section", "dp", "tensor"),
        ),
        out_specs=(
            P("section", "dp", "tensor"),
            P("section", "dp", "tensor"),
            P(("section", "tensor"), "dp"),
        ),
        check_vma=False,
    )
```

```python
import functools
import math

import jax
import jax.numpy as jnp
from jax import lax
from jax.experimental import pallas as pl
from jax.experimental.pallas import tpu as pltpu
from jax.sharding import PartitionSpec as P

HD = 128
TILE_TOK = 32
CORES = 2
MESH = pl.DeviceIdType.MESH
F32 = jnp.float32
BF16 = jnp.bfloat16
NT = (((1,), (1,)), ((), ()))
TN = (((0,), (0,)), ((), ()))
NN = (((1,), (0,)), ((), ()))


def dot(a, b, dims):
    return lax.dot_general(a, b, dims, preferred_element_type=F32)


def counts(n_s, n_y):
    near = (n_s - 1) + (n_y - 1)
    far = (n_s - 1) * (n_y - 1)
    chips = n_s * n_y
    gather_sends = 2 * near + 2 * far + 2 * chips
    scatter_sends = chips + 2 * far + 2 * near
    return gather_sends + scatter_sends


def kernel(
    n_s, n_y, block,
    gates_ref, tiles_ref, q_hbm, img_hbm, wk_hbm, wv_hbm, cot_hbm,
    att, dq, dimg_ref,
    w, q, cot, img, acc, kv, dk, dv, dkv_t, probs_t, ds_t,
    pair_out, pair_in, held, out_send, mid, last,
    local_sem, send_sem, img_sem, pair_sem, mid_sem, last_sem,
):
    s = lax.axis_index("section")
    t = lax.axis_index("tensor")
    y = t // CORES
    c = t % CORES
    n_t = n_y * CORES
    chunk = img_hbm.shape[0]
    half = chunk // 2
    slots = img_hbm.shape[1]
    width = wk_hbm.shape[1]
    tokens, columns = q.shape
    heads = columns // HD
    group = columns // width
    far = [(ds, dy) for ds in range(1, n_s) for dy in range(1, n_y)]
    near_s = [(ds, 0) for ds in range(1, n_s)]
    near_y = [(0, dy) for dy in range(1, n_y)]

    def place(ds, dy):
        return ds * n_y + dy

    def to(ds, dy, other=False):
        core = 1 - c if other else c
        return {
            "section": lax.rem(s + ds, n_s),
            "tensor": lax.rem(y + dy, n_y) * CORES + core,
        }

    def rows_of(ds, dy, core):
        chip = lax.rem(s + ds + n_s, n_s) * n_t + lax.rem(y + dy + n_y, n_y) * CORES
        return pl.ds(pl.multiple_of((chip + core) * chunk, chunk), chunk)

    sent = []

    def send(src, dst, sem, device):
        copy = pltpu.make_async_remote_copy(
            src_ref=src, dst_ref=dst, send_sem=send_sem.at[len(sent)],
            recv_sem=sem, device_id=device, device_id_type=MESH,
        )
        copy.start()
        sent.append(copy)

    def arrive(dst, sem):
        pltpu.make_async_remote_copy(
            src_ref=dst, dst_ref=dst, send_sem=send_sem.at[0],
            recv_sem=sem, device_id=to(0, 0, True), device_id_type=MESH,
        ).wait_recv()

    local = []

    def bring(src, dst):
        copy = pltpu.make_async_copy(src, dst, local_sem.at[len(local)])
        copy.start()
        local.append(copy)
        return copy

    barrier = pltpu.get_barrier_semaphore()
    partners = [to(0, 0, True)] + [to(ds, dy) for ds, dy in near_s + near_y]
    for device in partners:
        pl.semaphore_signal(barrier, inc=1, device_id=device, device_id_type=MESH)
    own = bring(img_hbm, img.at[0, 0])
    parts = 4
    depth = w.shape[0] // parts
    weights = []
    for i in range(parts):
        piece = pl.ds(i * depth, depth)
        weights.append(bring(wk_hbm.at[piece], w.at[piece, pl.ds(0, width)]))
        weights.append(bring(wv_hbm.at[piece], w.at[piece, pl.ds(width, width)]))
    text = [bring(q_hbm, q), bring(cot_hbm, cot)]
    pl.semaphore_wait(barrier, len(partners))

    def piece_of(ds, dy, core, h):
        return img.at[place(ds, dy), core, pl.ds(h * half, half)]

    def own_piece(h):
        return img_hbm.at[pl.ds(h * half, half)]

    for h in range(2):
        for ds, dy in near_s:
            send(own_piece(h), piece_of(ds, dy, 0, h), img_sem.at[place(ds, dy), 0, h], to(ds, dy))
        for ds, dy in near_y:
            send(own_piece(1 - h), piece_of(ds, dy, 0, 1 - h), img_sem.at[place(ds, dy), 0, 1 - h], to(ds, dy))
    for h in range(2):
        send(own_piece(h), piece_of(0, 0, 1, h), img_sem.at[0, 1, h], to(0, 0, True))

    def receive(ds, dy, core, h):
        arrive(piece_of(ds, dy, core, h), img_sem.at[place(ds, dy), core, h])

    def share(ds, dy, h):
        send(piece_of(ds, dy, 0, h), piece_of(ds, dy, 1, h), img_sem.at[place(ds, dy), 1, h], to(0, 0, True))

    def project(ds, dy, core, first=0, length=chunk):
        start = rows_of(-ds, -dy, 1 - c if core else c).start + first
        features = img[place(ds, dy), core, pl.ds(first, length)]
        acc[...] += dot(features, w[pl.ds(pl.multiple_of(start, half), length), :], TN)

    for ds, dy in near_s:
        receive(ds, dy, 0, 0)
        for _, ey in near_y:
            send(piece_of(ds, 0, 0, 0), piece_of(ds, ey, 0, 0), img_sem.at[place(ds, ey), 0, 0], to(0, ey))
        share(ds, dy, 0)
    for ds, dy in near_y:
        receive(ds, dy, 0, 1)
        for es, _ in near_s:
            send(piece_of(0, dy, 0, 1), piece_of(es, dy, 0, 1), img_sem.at[place(es, dy), 0, 1], to(es, 0))
        share(ds, dy, 1)
    acc[...] = jnp.zeros_like(acc)
    for copy in weights:
        copy.wait()
    own.wait()
    project(0, 0, 0)
    for h in range(2):
        receive(0, 0, 1, h)
    project(0, 0, 1)
    for copy in text:
        copy.wait()
    scale = jnp.tanh(jnp.full((1, HD), gates_ref[0], F32))
    for i in range(heads):
        part = pl.ds(i * HD, HD)
        cot[:, part] = (scale * cot[:, part].astype(F32)).astype(BF16)
    for ds, dy in near_s:
        receive(ds, dy, 0, 1)
        share(ds, dy, 1)
    for ds, dy in near_y:
        receive(ds, dy, 0, 0)
        share(ds, dy, 0)
    for ds, dy in near_s + near_y:
        project(ds, dy, 0)
    for ds, dy in near_s + near_y:
        for h in range(2):
            receive(ds, dy, 1, h)
        project(ds, dy, 1)
    for ds, dy in far:
        for h in range(2):
            receive(ds, dy, 0, h)
            share(ds, dy, h)
            project(ds, dy, 0, h * half, half)
    for ds, dy in far:
        for h in range(2):
            receive(ds, dy, 1, h)
            project(ds, dy, 1, h * half, half)

    kv[...] = acc[...].astype(BF16)
    dk[...] = jnp.zeros_like(dk)
    dv[...] = jnp.zeros_like(dv)
    valid = tiles_ref[0] * TILE_TOK
    factor = 1.0 / math.sqrt(HD)

    def lanes(i, offset=0):
        return pl.ds(pl.multiple_of(i * HD + offset, HD), HD)

    def attend(b, carry):
        first = b * block
        j = first // group
        key = kv[:, lanes(j)]
        value = kv[:, lanes(j, width)]
        allowed = lax.broadcasted_iota(jnp.int32, (slots, tokens), 0) < valid
        total_k = dk[:, lanes(j)]
        total_v = dv[:, lanes(j)]
        for i in range(block):
            query = q[:, lanes(first + i)]
            upstream = cot[:, lanes(first + i)]
            scores = jnp.where(allowed, dot(key, query, NT) * factor, -1e30)
            expo = jnp.exp(scores - jnp.max(scores, axis=0, keepdims=True))
            probs = expo * (1.0 / jnp.sum(expo, axis=0, keepdims=True))
            probs_b = probs.astype(BF16)
            d_probs = dot(value, upstream, NT)
            delta = jnp.sum(probs * d_probs, axis=0, keepdims=True)
            d_scores = (probs * (d_probs - delta) * factor).astype(BF16)
            total_v += dot(probs_b, upstream, NN)
            total_k += dot(d_scores, query, NN)
            probs_t[first + i] = probs_b
            ds_t[first + i] = d_scores
        dk[:, lanes(j)] = total_k
        dv[:, lanes(j)] = total_v
        return carry

    lax.fori_loop(0, heads // block, attend, 0, unroll=True)
    dkv_t[:width, :] = dk[...].astype(BF16).T
    dkv_t[width:, :] = dv[...].astype(BF16).T

    def finish(b, carry):
        first = b * block
        j = first // group
        key = kv[:, lanes(j)]
        value = kv[:, lanes(j, width)]
        for i in range(block):
            context = dot(probs_t[first + i], value, TN)
            att[:, lanes(first + i)] = (scale * context).astype(BF16)
            dq[:, lanes(first + i)] = dot(ds_t[first + i], key, TN).astype(BF16)
        return carry

    def term(ds, dy, core):
        rows = rows_of(ds, dy, core)
        return dot(w[rows, :], dkv_t[...], NN)

    def start_pair(ds, dy):
        k = place(ds, dy)
        pair_out[k] = term(ds, dy, 1 - c).astype(BF16)
        send(pair_out.at[k], pair_in.at[k], pair_sem.at[k], to(0, 0, True))
        held[k] = term(ds, dy, c)

    def end_pair(ds, dy):
        k = place(ds, dy)
        arrive(pair_in.at[k], pair_sem.at[k])
        total = held[k] + pair_in[k].astype(F32)
        if (ds, dy) in far:
            out_send[k] = total.astype(BF16)
            send(out_send.at[k, pl.ds(0, half)], mid.at[0, k], mid_sem.at[0, k], to(ds, 0))
            send(out_send.at[k, pl.ds(half, half)], mid.at[1, k], mid_sem.at[1, k], to(0, dy))
        else:
            held[k] = total
            if (ds, dy) != (0, 0):
                h = 0 if ds else 1
                pass_on(ds, dy, h)

    def pass_on(ds, dy, h):
        k = place(ds, dy)
        piece = pl.ds(h * half, half)
        out_send[k, piece] = held[k, piece].astype(BF16)
        send(out_send.at[k, piece], last.at[k, piece], last_sem.at[k, h], to(ds, dy))

    order = far + near_s + near_y + [(0, 0)]
    for n, target in enumerate(order):
        start_pair(*target)
        if n:
            end_pair(*order[n - 1])
    end_pair(*order[-1])
    blocks = heads // block
    lax.fori_loop(0, blocks // 2, finish, 0)
    for ds, dy in near_s + near_y:
        k = place(ds, dy)
        h = 1 if ds else 0
        piece = pl.ds(h * half, half)
        for es, ey in far:
            if (es == ds) if ds else (ey == dy):
                m = place(es, ey)
                arrive(mid.at[h, m], mid_sem.at[h, m])
                held[k, piece] += mid[h, m].astype(F32)
        pass_on(ds, dy, h)
    lax.fori_loop(blocks // 2, blocks, finish, 0)
    total = held[0]
    for ds, dy in near_s + near_y:
        k = place(ds, dy)
        for h in range(2):
            arrive(last.at[k, pl.ds(h * half, half)], last_sem.at[k, h])
        total += last[k].astype(F32)
    dimg_ref[...] = total.astype(BF16)
    for copy in sent:
        copy.wait_send()


def write_out(count, *refs):
    sem = refs[-1]
    copies = [pltpu.make_async_copy(refs[i], refs[count + i], sem.at[i]) for i in range(count)]
    for copy in copies:
        copy.start()
    for copy in copies:
        copy.wait()


def solution(mesh):
    n_s = mesh.shape["section"]
    n_t = mesh.shape["tensor"]
    n_y = n_t // CORES
    chips = n_s * n_y

    def shards(queries, image, w_key, w_value, gates, tiles, cotangent):
        text, upstream = queries[0], cotangent[0]
        weight_key, weight_value = w_key[0], w_value[0]
        tokens, columns = text.shape
        d, width = weight_key.shape
        chunk, slots = image.shape
        heads = columns // HD
        group = columns // width
        block = math.gcd(group, 8)
        half = chunk // 2
        smem = pl.BlockSpec(memory_space=pltpu.SMEM)
        vmem = pl.BlockSpec(memory_space=pltpu.VMEM)
        hbm = pl.BlockSpec(memory_space=pltpu.HBM)
        dma = pltpu.SemaphoreType.DMA
        results = pl.pallas_call(
            functools.partial(kernel, n_s, n_y, block),
            out_shape=(
                pltpu.VMEM((tokens, columns), BF16),
                pltpu.VMEM((tokens, columns), BF16),
                pltpu.VMEM((chunk, slots), BF16),
            ),
            in_specs=[smem, smem] + [hbm] * 5,
            out_specs=(vmem, vmem, vmem),
            scratch_shapes=[
                pltpu.VMEM((d, 2 * width), BF16),
                pltpu.VMEM((tokens, columns), BF16),
                pltpu.VMEM((tokens, columns), BF16),
                pltpu.VMEM((chips, CORES, chunk, slots), BF16),
                pltpu.VMEM((slots, 2 * width), F32),
                pltpu.VMEM((slots, 2 * width), BF16),
                pltpu.VMEM((slots, width), F32),
                pltpu.VMEM((slots, width), F32),
                pltpu.VMEM((2 * width, slots), BF16),
                pltpu.VMEM((heads, slots, tokens), BF16),
                pltpu.VMEM((heads, slots, tokens), BF16),
                pltpu.VMEM((chips, chunk, slots), BF16),
                pltpu.VMEM((chips, chunk, slots), BF16),
                pltpu.VMEM((chips, chunk, slots), F32),
                pltpu.VMEM((chips, chunk, slots), BF16),
                pltpu.VMEM((2, chips, half, slots), BF16),
                pltpu.VMEM((chips, chunk, slots), BF16),
                dma((11,)),
                dma((counts(n_s, n_y),)),
                dma((chips, CORES, 2)),
                dma((chips,)),
                dma((2, chips)),
                dma((chips, 2)),
            ],
            compiler_params=pltpu.CompilerParams(
                collective_id=0, has_side_effects=True, vmem_limit_bytes=60 * 1024 * 1024
            ),
            cost_estimate=pl.CostEstimate(
                flops=8 * d * width * slots + 12 * tokens * columns * slots,
                bytes_accessed=4 * d * width + 8 * tokens * columns,
                transcendentals=heads * tokens * slots,
            ),
        )(gates, tiles, text, image, weight_key, weight_value, upstream)
        attended, d_query, d_image = pl.pallas_call(
            functools.partial(write_out, len(results)),
            out_shape=tuple(jax.ShapeDtypeStruct(a.shape, a.dtype) for a in results),
            in_specs=[vmem] * len(results),
            out_specs=tuple(hbm for _ in results),
            scratch_shapes=[dma((len(results),))],
            compiler_params=pltpu.CompilerParams(vmem_limit_bytes=8 * 1024 * 1024),
        )(*results)
        return attended[None], d_query[None], d_image

    return jax.shard_map(
        shards,
        mesh=mesh,
        in_specs=(
            P("section", "dp", "tensor"),
            P(("section", "tensor"), "dp"),
            P("section", None, "tensor"),
            P("section", None, "tensor"),
            P("section"),
            P("dp"),
            P("section", "dp", "tensor"),
        ),
        out_specs=(
            P("section", "dp", "tensor"),
            P("section", "dp", "tensor"),
            P(("section", "tensor"), "dp"),
        ),
        check_vma=False,
    )
```

```python
import functools
import math

import jax
import jax.numpy as jnp
from jax import lax
from jax.experimental import pallas as pl
from jax.experimental.pallas import tpu as pltpu
from jax.sharding import PartitionSpec as P

HD = 128
TILE_TOK = 32
CORES = 2
MESH = pl.DeviceIdType.MESH
F32 = jnp.float32
BF16 = jnp.bfloat16
NT = (((1,), (1,)), ((), ()))
TN = (((0,), (0,)), ((), ()))
NN = (((1,), (0,)), ((), ()))


def dot(a, b, dims):
    return lax.dot_general(a, b, dims, preferred_element_type=F32)


def counts(n_s, n_y):
    near = (n_s - 1) + (n_y - 1)
    far = (n_s - 1) * (n_y - 1)
    chips = n_s * n_y
    gather_sends = 2 * near + 2 * far + 2 * chips
    scatter_sends = 2 * chips + 2 * far + 2 * near
    return gather_sends + scatter_sends


def kernel(
    n_s, n_y, block,
    gates_ref, tiles_ref, q_hbm, img_hbm, wk_hbm, wv_hbm, cot_hbm,
    att, dq, dimg_ref,
    w, q, cot, q_t, cot_t, img, acc, kv, dk, dv, dkv_t, probs_t, ds_t,
    pair_out, pair_in, held, out_send, mid, last,
    local_sem, send_sem, img_sem, pair_sem, mid_sem, last_sem,
):
    s = lax.axis_index("section")
    t = lax.axis_index("tensor")
    y = t // CORES
    c = t % CORES
    n_t = n_y * CORES
    chunk = img_hbm.shape[0]
    half = chunk // 2
    slots = img_hbm.shape[1]
    width = wk_hbm.shape[1]
    tokens, columns = q.shape
    heads = columns // HD
    group = columns // width
    far = [(ds, dy) for ds in range(1, n_s) for dy in range(1, n_y)]
    near_s = [(ds, 0) for ds in range(1, n_s)]
    near_y = [(0, dy) for dy in range(1, n_y)]

    def place(ds, dy):
        return ds * n_y + dy

    def to(ds, dy, other=False):
        core = 1 - c if other else c
        return {
            "section": lax.rem(s + ds, n_s),
            "tensor": lax.rem(y + dy, n_y) * CORES + core,
        }

    def rows_of(ds, dy, core):
        chip = lax.rem(s + ds + n_s, n_s) * n_t + lax.rem(y + dy + n_y, n_y) * CORES
        return pl.ds(pl.multiple_of((chip + core) * chunk, chunk), chunk)

    sent = []

    def send(src, dst, sem, device):
        copy = pltpu.make_async_remote_copy(
            src_ref=src, dst_ref=dst, send_sem=send_sem.at[len(sent)],
            recv_sem=sem, device_id=device, device_id_type=MESH,
        )
        copy.start()
        sent.append(copy)

    def arrive(dst, sem):
        pltpu.make_async_remote_copy(
            src_ref=dst, dst_ref=dst, send_sem=send_sem.at[0],
            recv_sem=sem, device_id=to(0, 0, True), device_id_type=MESH,
        ).wait_recv()

    local = []

    def bring(src, dst):
        copy = pltpu.make_async_copy(src, dst, local_sem.at[len(local)])
        copy.start()
        local.append(copy)
        return copy

    barrier = pltpu.get_barrier_semaphore()
    partners = [to(0, 0, True)] + [to(ds, dy) for ds, dy in near_s + near_y]
    for device in partners:
        pl.semaphore_signal(barrier, inc=1, device_id=device, device_id_type=MESH)
    text = [bring(q_hbm, q), bring(cot_hbm, cot)]
    own = bring(img_hbm, img.at[0, 0])
    parts = 4
    depth = w.shape[0] // parts
    weights = []
    for i in range(parts):
        piece = pl.ds(i * depth, depth)
        weights.append(bring(wk_hbm.at[piece], w.at[piece, pl.ds(0, width)]))
        weights.append(bring(wv_hbm.at[piece], w.at[piece, pl.ds(width, width)]))
    pl.semaphore_wait(barrier, len(partners))

    def piece_of(ds, dy, core, h):
        return img.at[place(ds, dy), core, pl.ds(h * half, half)]

    def own_piece(h):
        return img_hbm.at[pl.ds(h * half, half)]

    for h in range(2):
        for ds, dy in near_s:
            send(own_piece(h), piece_of(ds, dy, 0, h), img_sem.at[place(ds, dy), 0, h], to(ds, dy))
        for ds, dy in near_y:
            send(own_piece(1 - h), piece_of(ds, dy, 0, 1 - h), img_sem.at[place(ds, dy), 0, 1 - h], to(ds, dy))
    for h in range(2):
        send(own_piece(h), piece_of(0, 0, 1, h), img_sem.at[0, 1, h], to(0, 0, True))

    def receive(ds, dy, core, h):
        arrive(piece_of(ds, dy, core, h), img_sem.at[place(ds, dy), core, h])

    def share(ds, dy, h):
        send(piece_of(ds, dy, 0, h), piece_of(ds, dy, 1, h), img_sem.at[place(ds, dy), 1, h], to(0, 0, True))

    def project(ds, dy, core, first=0, length=chunk):
        start = rows_of(-ds, -dy, 1 - c if core else c).start + first
        features = img[place(ds, dy), core, pl.ds(first, length)]
        acc[...] += dot(features, w[pl.ds(pl.multiple_of(start, half), length), :], TN)

    for copy in text:
        copy.wait()
    scale = jnp.tanh(jnp.full((1, HD), gates_ref[0], F32))
    for i in range(heads):
        part = pl.ds(i * HD, HD)
        upstream = (scale * cot[:, part].astype(F32)).astype(BF16)
        cot[:, part] = upstream
        cot_t[part, :] = upstream.T
        q_t[part, :] = q[:, part].T
    acc[...] = jnp.zeros_like(acc)
    for copy in weights:
        copy.wait()
    own.wait()
    project(0, 0, 0)
    for ds, dy in near_s:
        receive(ds, dy, 0, 0)
        for _, ey in near_y:
            send(piece_of(ds, 0, 0, 0), piece_of(ds, ey, 0, 0), img_sem.at[place(ds, ey), 0, 0], to(0, ey))
        share(ds, dy, 0)
    for ds, dy in near_y:
        receive(ds, dy, 0, 1)
        for es, _ in near_s:
            send(piece_of(0, dy, 0, 1), piece_of(es, dy, 0, 1), img_sem.at[place(es, dy), 0, 1], to(es, 0))
        share(ds, dy, 1)
    for h in range(2):
        receive(0, 0, 1, h)
    project(0, 0, 1)
    for ds, dy in near_s:
        receive(ds, dy, 0, 1)
        share(ds, dy, 1)
    for ds, dy in near_y:
        receive(ds, dy, 0, 0)
        share(ds, dy, 0)
    for ds, dy in near_s + near_y:
        project(ds, dy, 0)
    for ds, dy in near_s + near_y:
        for h in range(2):
            receive(ds, dy, 1, h)
        project(ds, dy, 1)
    for ds, dy in far:
        for h in range(2):
            receive(ds, dy, 0, h)
            share(ds, dy, h)
            project(ds, dy, 0, h * half, half)
    for ds, dy in far:
        for h in range(2):
            receive(ds, dy, 1, h)
            project(ds, dy, 1, h * half, half)

    kv[...] = acc[...].astype(BF16)
    dk[...] = jnp.zeros_like(dk)
    dv[...] = jnp.zeros_like(dv)
    valid = tiles_ref[0] * TILE_TOK
    factor = 1.0 / math.sqrt(HD)

    def lanes(i, offset=0):
        return pl.ds(pl.multiple_of(i * HD + offset, HD), HD)

    def attend(b, carry):
        first = b * block
        j = first // group
        key = kv[:, lanes(j)]
        value = kv[:, lanes(j, width)]
        allowed = lax.broadcasted_iota(jnp.int32, (slots, tokens), 0) < valid
        total_k = dk[:, lanes(j)]
        total_v = dv[:, lanes(j)]
        for i in range(block):
            query = q[:, lanes(first + i)]
            upstream = cot[:, lanes(first + i)]
            scores = jnp.where(allowed, dot(key, q_t[lanes(first + i), :], NN) * factor, -1e30)
            expo = jnp.exp(scores - jnp.max(scores, axis=0, keepdims=True))
            probs = expo * (1.0 / jnp.sum(expo, axis=0, keepdims=True))
            probs_b = probs.astype(BF16)
            d_probs = dot(value, cot_t[lanes(first + i), :], NN)
            delta = jnp.sum(probs * d_probs, axis=0, keepdims=True)
            d_scores = (probs * (d_probs - delta) * factor).astype(BF16)
            total_v += dot(probs_b, upstream, NN)
            total_k += dot(d_scores, query, NN)
            probs_t[first + i] = probs_b
            ds_t[first + i] = d_scores
        dk[:, lanes(j)] = total_k
        dv[:, lanes(j)] = total_v
        return carry

    lax.fori_loop(0, heads // block, attend, 0, unroll=True)
    dkv_t[:width, :] = dk[...].astype(BF16).T
    dkv_t[width:, :] = dv[...].astype(BF16).T

    def finish(b, carry):
        first = b * block
        j = first // group
        key = kv[:, lanes(j)]
        value = kv[:, lanes(j, width)]
        for i in range(block):
            context = dot(probs_t[first + i], value, TN)
            att[:, lanes(first + i)] = (scale * context).astype(BF16)
            dq[:, lanes(first + i)] = dot(ds_t[first + i], key, TN).astype(BF16)
        return carry

    def term(ds, dy, core, h):
        start = rows_of(ds, dy, core).start + h * half
        return dot(w[pl.ds(pl.multiple_of(start, half), half), :], dkv_t[...], NN)

    def start_pair(ds, dy, h):
        k = place(ds, dy)
        piece = pl.ds(h * half, half)
        pair_out[k, piece] = term(ds, dy, 1 - c, h).astype(BF16)
        send(pair_out.at[k, piece], pair_in.at[k, piece], pair_sem.at[k, h], to(0, 0, True))
        held[k, piece] = term(ds, dy, c, h)

    def end_pair(ds, dy, h):
        k = place(ds, dy)
        piece = pl.ds(h * half, half)
        arrive(pair_in.at[k, piece], pair_sem.at[k, h])
        total = held[k, piece] + pair_in[k, piece].astype(F32)
        if (ds, dy) in far:
            out_send[k, piece] = total.astype(BF16)
            send(out_send.at[k, piece], mid.at[h, k], mid_sem.at[h, k], to(0, dy) if h else to(ds, 0))
        elif (ds, dy, h) in direct:
            out_send[k, piece] = total.astype(BF16)
            send(out_send.at[k, piece], last.at[k, piece], last_sem.at[k, h], to(ds, dy))
        else:
            held[k, piece] = total

    direct = [(ds, dy, 0) for ds, dy in near_s] + [(ds, dy, 1) for ds, dy in near_y]
    joined = [(ds, dy, 1) for ds, dy in near_s] + [(ds, dy, 0) for ds, dy in near_y]
    order = [(ds, dy, h) for ds, dy in far for h in range(2)] + direct + joined + [(0, 0, 0), (0, 0, 1)]
    lag = min(3, len(order))
    for n, unit in enumerate(order):
        start_pair(*unit)
        if n >= lag:
            end_pair(*order[n - lag])
    for unit in order[len(order) - lag:]:
        end_pair(*unit)
    blocks = heads // block
    lax.fori_loop(0, blocks // 2, finish, 0)
    for ds, dy, h in joined:
        k = place(ds, dy)
        piece = pl.ds(h * half, half)
        total = held[k, piece]
        for es, ey in far:
            if (es == ds) if ds else (ey == dy):
                m = place(es, ey)
                arrive(mid.at[h, m], mid_sem.at[h, m])
                total += mid[h, m].astype(F32)
        out_send[k, piece] = total.astype(BF16)
        send(out_send.at[k, piece], last.at[k, piece], last_sem.at[k, h], to(ds, dy))
    lax.fori_loop(blocks // 2, blocks, finish, 0)
    total = held[0]
    for ds, dy in near_s + near_y:
        k = place(ds, dy)
        for h in range(2):
            arrive(last.at[k, pl.ds(h * half, half)], last_sem.at[k, h])
        total += last[k].astype(F32)
    dimg_ref[...] = total.astype(BF16)
    for copy in sent:
        copy.wait_send()


def write_out(count, *refs):
    sem = refs[-1]
    copies = [pltpu.make_async_copy(refs[i], refs[count + i], sem.at[i]) for i in range(count)]
    for copy in copies:
        copy.start()
    for copy in copies:
        copy.wait()


def solution(mesh):
    n_s = mesh.shape["section"]
    n_t = mesh.shape["tensor"]
    n_y = n_t // CORES
    chips = n_s * n_y

    def shards(queries, image, w_key, w_value, gates, tiles, cotangent):
        text, upstream = queries[0], cotangent[0]
        weight_key, weight_value = w_key[0], w_value[0]
        tokens, columns = text.shape
        d, width = weight_key.shape
        chunk, slots = image.shape
        heads = columns // HD
        group = columns // width
        block = math.gcd(group, 8)
        half = chunk // 2
        smem = pl.BlockSpec(memory_space=pltpu.SMEM)
        vmem = pl.BlockSpec(memory_space=pltpu.VMEM)
        hbm = pl.BlockSpec(memory_space=pltpu.HBM)
        dma = pltpu.SemaphoreType.DMA
        results = pl.pallas_call(
            functools.partial(kernel, n_s, n_y, block),
            out_shape=(
                pltpu.VMEM((tokens, columns), BF16),
                pltpu.VMEM((tokens, columns), BF16),
                pltpu.VMEM((chunk, slots), BF16),
            ),
            in_specs=[smem, smem] + [hbm] * 5,
            out_specs=(vmem, vmem, vmem),
            scratch_shapes=[
                pltpu.VMEM((d, 2 * width), BF16),
                pltpu.VMEM((tokens, columns), BF16),
                pltpu.VMEM((tokens, columns), BF16),
                pltpu.VMEM((columns, tokens), BF16),
                pltpu.VMEM((columns, tokens), BF16),
                pltpu.VMEM((chips, CORES, chunk, slots), BF16),
                pltpu.VMEM((slots, 2 * width), F32),
                pltpu.VMEM((slots, 2 * width), BF16),
                pltpu.VMEM((slots, width), F32),
                pltpu.VMEM((slots, width), F32),
                pltpu.VMEM((2 * width, slots), BF16),
                pltpu.VMEM((heads, slots, tokens), BF16),
                pltpu.VMEM((heads, slots, tokens), BF16),
                pltpu.VMEM((chips, chunk, slots), BF16),
                pltpu.VMEM((chips, chunk, slots), BF16),
                pltpu.VMEM((chips, chunk, slots), F32),
                pltpu.VMEM((chips, chunk, slots), BF16),
                pltpu.VMEM((2, chips, half, slots), BF16),
                pltpu.VMEM((chips, chunk, slots), BF16),
                dma((11,)),
                dma((counts(n_s, n_y),)),
                dma((chips, CORES, 2)),
                dma((chips, 2)),
                dma((2, chips)),
                dma((chips, 2)),
            ],
            compiler_params=pltpu.CompilerParams(
                collective_id=0, has_side_effects=True, vmem_limit_bytes=60 * 1024 * 1024
            ),
            cost_estimate=pl.CostEstimate(
                flops=8 * d * width * slots + 12 * tokens * columns * slots,
                bytes_accessed=4 * d * width + 8 * tokens * columns,
                transcendentals=heads * tokens * slots,
            ),
        )(gates, tiles, text, image, weight_key, weight_value, upstream)
        attended, d_query, d_image = pl.pallas_call(
            functools.partial(write_out, len(results)),
            out_shape=tuple(jax.ShapeDtypeStruct(a.shape, a.dtype) for a in results),
            in_specs=[vmem] * len(results),
            out_specs=tuple(hbm for _ in results),
            scratch_shapes=[dma((len(results),))],
            compiler_params=pltpu.CompilerParams(vmem_limit_bytes=8 * 1024 * 1024),
        )(*results)
        return attended[None], d_query[None], d_image

    return jax.shard_map(
        shards,
        mesh=mesh,
        in_specs=(
            P("section", "dp", "tensor"),
            P(("section", "tensor"), "dp"),
            P("section", None, "tensor"),
            P("section", None, "tensor"),
            P("section"),
            P("dp"),
            P("section", "dp", "tensor"),
        ),
        out_specs=(
            P("section", "dp", "tensor"),
            P("section", "dp", "tensor"),
            P(("section", "tensor"), "dp"),
        ),
        check_vma=False,
    )
```

```python
import functools
import math

import jax
import jax.numpy as jnp
from jax import lax
from jax.experimental import pallas as pl
from jax.experimental.pallas import tpu as pltpu
from jax.sharding import PartitionSpec as P

HD = 128
TILE_TOK = 32
CORES = 2
MESH = pl.DeviceIdType.MESH
F32 = jnp.float32
BF16 = jnp.bfloat16
NT = (((1,), (1,)), ((), ()))
TN = (((0,), (0,)), ((), ()))
NN = (((1,), (0,)), ((), ()))


def dot(a, b, dims):
    return lax.dot_general(a, b, dims, preferred_element_type=F32)


def counts(n_s, n_y):
    near = (n_s - 1) + (n_y - 1)
    far = (n_s - 1) * (n_y - 1)
    chips = n_s * n_y
    gather_sends = 2 * near + 2 * far + 2 * chips
    scatter_sends = 2 * chips + 2 * far + 2 * near
    return gather_sends + scatter_sends


def kernel(
    n_s, n_y, block,
    gates_ref, tiles_ref, q_hbm, img_hbm, wk_hbm, wv_hbm, cot_hbm,
    att, dq, dimg_ref,
    w, q, cot, img, acc, kv, dk, dv, dkv_t, probs_t, ds_t,
    pair_out, pair_in, held, out_send, mid, last,
    local_sem, send_sem, img_sem, pair_sem, mid_sem, last_sem,
):
    s = lax.axis_index("section")
    t = lax.axis_index("tensor")
    y = t // CORES
    c = t % CORES
    n_t = n_y * CORES
    chunk = img_hbm.shape[0]
    half = chunk // 2
    slots = img_hbm.shape[1]
    width = wk_hbm.shape[1]
    tokens, columns = q.shape
    heads = columns // HD
    group = columns // width
    far = [(ds, dy) for ds in range(1, n_s) for dy in range(1, n_y)]
    near_s = [(ds, 0) for ds in range(1, n_s)]
    near_y = [(0, dy) for dy in range(1, n_y)]

    def place(ds, dy):
        return ds * n_y + dy

    def to(ds, dy, other=False):
        core = 1 - c if other else c
        return {
            "section": lax.rem(s + ds, n_s),
            "tensor": lax.rem(y + dy, n_y) * CORES + core,
        }

    def rows_of(ds, dy, core):
        chip = lax.rem(s + ds + n_s, n_s) * n_t + lax.rem(y + dy + n_y, n_y) * CORES
        return pl.ds(pl.multiple_of((chip + core) * chunk, chunk), chunk)

    sent = []

    def send(src, dst, sem, device):
        copy = pltpu.make_async_remote_copy(
            src_ref=src, dst_ref=dst, send_sem=send_sem.at[len(sent)],
            recv_sem=sem, device_id=device, device_id_type=MESH,
        )
        copy.start()
        sent.append(copy)

    def arrive(dst, sem):
        pltpu.make_async_remote_copy(
            src_ref=dst, dst_ref=dst, send_sem=send_sem.at[0],
            recv_sem=sem, device_id=to(0, 0, True), device_id_type=MESH,
        ).wait_recv()

    local = []

    def bring(src, dst):
        copy = pltpu.make_async_copy(src, dst, local_sem.at[len(local)])
        copy.start()
        local.append(copy)
        return copy

    barrier = pltpu.get_barrier_semaphore()
    partners = [to(0, 0, True)] + [to(ds, dy) for ds, dy in near_s + near_y]
    for device in partners:
        pl.semaphore_signal(barrier, inc=1, device_id=device, device_id_type=MESH)
    text = [bring(q_hbm, q), bring(cot_hbm, cot)]
    own = bring(img_hbm, img.at[0, 0])
    parts = 4
    depth = w.shape[0] // parts
    weights = []
    for i in range(parts):
        piece = pl.ds(i * depth, depth)
        weights.append(bring(wk_hbm.at[piece], w.at[piece, pl.ds(0, width)]))
        weights.append(bring(wv_hbm.at[piece], w.at[piece, pl.ds(width, width)]))
    pl.semaphore_wait(barrier, len(partners))

    def piece_of(ds, dy, core, h):
        return img.at[place(ds, dy), core, pl.ds(h * half, half)]

    def own_piece(h):
        return img_hbm.at[pl.ds(h * half, half)]

    def spread(h):
        for ds, dy in near_s:
            send(own_piece(h), piece_of(ds, dy, 0, h), img_sem.at[place(ds, dy), 0, h], to(ds, dy))
        for ds, dy in near_y:
            send(own_piece(1 - h), piece_of(ds, dy, 0, 1 - h), img_sem.at[place(ds, dy), 0, 1 - h], to(ds, dy))

    spread(0)
    for h in range(2):
        send(own_piece(h), piece_of(0, 0, 1, h), img_sem.at[0, 1, h], to(0, 0, True))
    for copy in text:
        copy.wait()
    scale = jnp.tanh(jnp.full((1, HD), gates_ref[0], F32))
    for i in range(heads):
        part = pl.ds(i * HD, HD)
        cot[:, part] = (scale * cot[:, part].astype(F32)).astype(BF16)
    spread(1)

    def receive(ds, dy, core, h):
        arrive(piece_of(ds, dy, core, h), img_sem.at[place(ds, dy), core, h])

    def share(ds, dy, h):
        send(piece_of(ds, dy, 0, h), piece_of(ds, dy, 1, h), img_sem.at[place(ds, dy), 1, h], to(0, 0, True))

    def project(ds, dy, core, first=0, length=chunk):
        start = rows_of(-ds, -dy, 1 - c if core else c).start + first
        features = img[place(ds, dy), core, pl.ds(first, length)]
        acc[...] += dot(features, w[pl.ds(pl.multiple_of(start, half), length), :], TN)

    for ds, dy in near_s:
        receive(ds, dy, 0, 0)
        for _, ey in near_y:
            send(piece_of(ds, 0, 0, 0), piece_of(ds, ey, 0, 0), img_sem.at[place(ds, ey), 0, 0], to(0, ey))
        share(ds, dy, 0)
    for ds, dy in near_y:
        receive(ds, dy, 0, 1)
        for es, _ in near_s:
            send(piece_of(0, dy, 0, 1), piece_of(es, dy, 0, 1), img_sem.at[place(es, dy), 0, 1], to(es, 0))
        share(ds, dy, 1)
    acc[...] = jnp.zeros_like(acc)
    for copy in weights:
        copy.wait()
    own.wait()
    project(0, 0, 0)
    for h in range(2):
        receive(0, 0, 1, h)
    project(0, 0, 1)
    for ds, dy in near_s:
        receive(ds, dy, 0, 1)
        share(ds, dy, 1)
    for ds, dy in near_y:
        receive(ds, dy, 0, 0)
        share(ds, dy, 0)
    for ds, dy in near_s + near_y:
        project(ds, dy, 0)
    for ds, dy in near_s + near_y:
        for h in range(2):
            receive(ds, dy, 1, h)
        project(ds, dy, 1)
    for ds, dy in far:
        for h in range(2):
            receive(ds, dy, 0, h)
            share(ds, dy, h)
            project(ds, dy, 0, h * half, half)
    for ds, dy in far:
        for h in range(2):
            receive(ds, dy, 1, h)
            project(ds, dy, 1, h * half, half)

    kv[...] = acc[...].astype(BF16)
    dk[...] = jnp.zeros_like(dk)
    dv[...] = jnp.zeros_like(dv)
    valid = tiles_ref[0] * TILE_TOK
    factor = 1.0 / math.sqrt(HD)

    def lanes(i, offset=0):
        return pl.ds(pl.multiple_of(i * HD + offset, HD), HD)

    def attend(b, carry):
        first = b * block
        j = first // group
        key = kv[:, lanes(j)]
        value = kv[:, lanes(j, width)]
        allowed = lax.broadcasted_iota(jnp.int32, (slots, tokens), 0) < valid
        total_k = dk[:, lanes(j)]
        total_v = dv[:, lanes(j)]
        for i in range(block):
            query = q[:, lanes(first + i)]
            upstream = cot[:, lanes(first + i)]
            scores = jnp.where(allowed, dot(key, query, NT) * factor, -1e30)
            expo = jnp.exp(scores - jnp.max(scores, axis=0, keepdims=True))
            probs = expo * (1.0 / jnp.sum(expo, axis=0, keepdims=True))
            probs_b = probs.astype(BF16)
            d_probs = dot(value, upstream, NT)
            delta = jnp.sum(probs * d_probs, axis=0, keepdims=True)
            d_scores = (probs * (d_probs - delta) * factor).astype(BF16)
            total_v += dot(probs_b, upstream, NN)
            total_k += dot(d_scores, query, NN)
            probs_t[first + i] = probs_b
            ds_t[first + i] = d_scores
        dk[:, lanes(j)] = total_k
        dv[:, lanes(j)] = total_v
        return carry

    lax.fori_loop(0, heads // block, attend, 0, unroll=True)
    dkv_t[:width, :] = dk[...].astype(BF16).T
    dkv_t[width:, :] = dv[...].astype(BF16).T

    def finish(b, carry):
        first = b * block
        j = first // group
        key = kv[:, lanes(j)]
        value = kv[:, lanes(j, width)]
        for i in range(block):
            context = dot(probs_t[first + i], value, TN)
            att[:, lanes(first + i)] = (scale * context).astype(BF16)
            dq[:, lanes(first + i)] = dot(ds_t[first + i], key, TN).astype(BF16)
        return carry

    def term(ds, dy, core, h):
        start = rows_of(ds, dy, core).start + h * half
        return dot(w[pl.ds(pl.multiple_of(start, half), half), :], dkv_t[...], NN)

    def start_pair(ds, dy, h):
        k = place(ds, dy)
        piece = pl.ds(h * half, half)
        pair_out[k, piece] = term(ds, dy, 1 - c, h).astype(BF16)
        send(pair_out.at[k, piece], pair_in.at[k, piece], pair_sem.at[k, h], to(0, 0, True))
        held[k, piece] = term(ds, dy, c, h)

    def end_pair(ds, dy, h):
        k = place(ds, dy)
        piece = pl.ds(h * half, half)
        arrive(pair_in.at[k, piece], pair_sem.at[k, h])
        total = held[k, piece] + pair_in[k, piece].astype(F32)
        if (ds, dy) in far:
            out_send[k, piece] = total.astype(BF16)
            send(out_send.at[k, piece], mid.at[h, k], mid_sem.at[h, k], to(0, dy) if h else to(ds, 0))
        elif (ds, dy, h) in direct:
            out_send[k, piece] = total.astype(BF16)
            send(out_send.at[k, piece], last.at[k, piece], last_sem.at[k, h], to(ds, dy))
        else:
            held[k, piece] = total

    direct = [(ds, dy, 0) for ds, dy in near_s] + [(ds, dy, 1) for ds, dy in near_y]
    joined = [(ds, dy, 1) for ds, dy in near_s] + [(ds, dy, 0) for ds, dy in near_y]
    order = [(ds, dy, h) for ds, dy in far for h in range(2)] + joined + [(0, 0, 0), (0, 0, 1)] + direct
    lag = min(3, len(order))
    for n, unit in enumerate(order):
        start_pair(*unit)
        if n >= lag:
            end_pair(*order[n - lag])
    for unit in order[len(order) - lag:]:
        end_pair(*unit)
    blocks = heads // block
    lax.fori_loop(0, blocks // 2, finish, 0)
    for ds, dy, h in joined:
        k = place(ds, dy)
        piece = pl.ds(h * half, half)
        total = held[k, piece]
        for es, ey in far:
            if (es == ds) if ds else (ey == dy):
                m = place(es, ey)
                arrive(mid.at[h, m], mid_sem.at[h, m])
                total += mid[h, m].astype(F32)
        out_send[k, piece] = total.astype(BF16)
        send(out_send.at[k, piece], last.at[k, piece], last_sem.at[k, h], to(ds, dy))
    lax.fori_loop(blocks // 2, blocks, finish, 0)
    total = held[0]
    for ds, dy in near_s + near_y:
        k = place(ds, dy)
        for h in range(2):
            arrive(last.at[k, pl.ds(h * half, half)], last_sem.at[k, h])
        total += last[k].astype(F32)
    dimg_ref[...] = total.astype(BF16)
    for copy in sent:
        copy.wait_send()


def write_out(count, parts, *refs):
    sem = refs[-1]
    copies = []
    for i in range(count):
        rows = refs[i].shape[0] // parts
        for part in range(parts):
            piece = pl.ds(part * rows, rows)
            copies.append(pltpu.make_async_copy(refs[i].at[piece], refs[count + i].at[piece], sem.at[i, part]))
    for copy in copies:
        copy.start()
    for copy in copies:
        copy.wait()


def solution(mesh):
    n_s = mesh.shape["section"]
    n_t = mesh.shape["tensor"]
    n_y = n_t // CORES
    chips = n_s * n_y

    def shards(queries, image, w_key, w_value, gates, tiles, cotangent):
        text, upstream = queries[0], cotangent[0]
        weight_key, weight_value = w_key[0], w_value[0]
        tokens, columns = text.shape
        d, width = weight_key.shape
        chunk, slots = image.shape
        heads = columns // HD
        group = columns // width
        block = math.gcd(group, 8)
        half = chunk // 2
        smem = pl.BlockSpec(memory_space=pltpu.SMEM)
        vmem = pl.BlockSpec(memory_space=pltpu.VMEM)
        hbm = pl.BlockSpec(memory_space=pltpu.HBM)
        dma = pltpu.SemaphoreType.DMA
        results = pl.pallas_call(
            functools.partial(kernel, n_s, n_y, block),
            out_shape=(
                pltpu.VMEM((tokens, columns), BF16),
                pltpu.VMEM((tokens, columns), BF16),
                pltpu.VMEM((chunk, slots), BF16),
            ),
            in_specs=[smem, smem] + [hbm] * 5,
            out_specs=(vmem, vmem, vmem),
            scratch_shapes=[
                pltpu.VMEM((d, 2 * width), BF16),
                pltpu.VMEM((tokens, columns), BF16),
                pltpu.VMEM((tokens, columns), BF16),
                pltpu.VMEM((chips, CORES, chunk, slots), BF16),
                pltpu.VMEM((slots, 2 * width), F32),
                pltpu.VMEM((slots, 2 * width), BF16),
                pltpu.VMEM((slots, width), F32),
                pltpu.VMEM((slots, width), F32),
                pltpu.VMEM((2 * width, slots), BF16),
                pltpu.VMEM((heads, slots, tokens), BF16),
                pltpu.VMEM((heads, slots, tokens), BF16),
                pltpu.VMEM((chips, chunk, slots), BF16),
                pltpu.VMEM((chips, chunk, slots), BF16),
                pltpu.VMEM((chips, chunk, slots), F32),
                pltpu.VMEM((chips, chunk, slots), BF16),
                pltpu.VMEM((2, chips, half, slots), BF16),
                pltpu.VMEM((chips, chunk, slots), BF16),
                dma((11,)),
                dma((counts(n_s, n_y),)),
                dma((chips, CORES, 2)),
                dma((chips, 2)),
                dma((2, chips)),
                dma((chips, 2)),
            ],
            compiler_params=pltpu.CompilerParams(
                collective_id=0, has_side_effects=True, vmem_limit_bytes=60 * 1024 * 1024
            ),
            cost_estimate=pl.CostEstimate(
                flops=8 * d * width * slots + 12 * tokens * columns * slots,
                bytes_accessed=4 * d * width + 8 * tokens * columns,
                transcendentals=heads * tokens * slots,
            ),
        )(gates, tiles, text, image, weight_key, weight_value, upstream)
        attended, d_query, d_image = pl.pallas_call(
            functools.partial(write_out, len(results), 4),
            out_shape=tuple(jax.ShapeDtypeStruct(a.shape, a.dtype) for a in results),
            in_specs=[vmem] * len(results),
            out_specs=tuple(hbm for _ in results),
            scratch_shapes=[dma((len(results), 4))],
            compiler_params=pltpu.CompilerParams(vmem_limit_bytes=8 * 1024 * 1024),
        )(*results)
        return attended[None], d_query[None], d_image

    return jax.shard_map(
        shards,
        mesh=mesh,
        in_specs=(
            P("section", "dp", "tensor"),
            P(("section", "tensor"), "dp"),
            P("section", None, "tensor"),
            P("section", None, "tensor"),
            P("section"),
            P("dp"),
            P("section", "dp", "tensor"),
        ),
        out_specs=(
            P("section", "dp", "tensor"),
            P("section", "dp", "tensor"),
            P(("section", "tensor"), "dp"),
        ),
        check_vma=False,
    )
```

```python
import functools
import math

import jax
import jax.numpy as jnp
from jax import lax
from jax.experimental import pallas as pl
from jax.experimental.pallas import tpu as pltpu
from jax.sharding import PartitionSpec as P

HD = 128
TILE_TOK = 32
CORES = 2
MESH = pl.DeviceIdType.MESH
F32 = jnp.float32
BF16 = jnp.bfloat16
NT = (((1,), (1,)), ((), ()))
TN = (((0,), (0,)), ((), ()))
NN = (((1,), (0,)), ((), ()))


def dot(a, b, dims):
    return lax.dot_general(a, b, dims, preferred_element_type=F32)


def counts(n_s, n_y):
    near = (n_s - 1) + (n_y - 1)
    far = (n_s - 1) * (n_y - 1)
    chips = n_s * n_y
    gather_sends = 2 * near + 2 * far + 2 * chips
    scatter_sends = chips + 2 * far + 2 * near
    return gather_sends + scatter_sends


def kernel(
    n_s, n_y, block,
    gates_ref, tiles_ref, q_hbm, img_hbm, wk_hbm, wv_hbm, cot_hbm,
    att, dq, dimg_ref,
    w, q, cot, img, acc, kv, dk, dv, dkv_t, probs_t, ds_t,
    pair_out, pair_in, held, out_send, mid, last,
    local_sem, send_sem, img_sem, pair_sem, mid_sem, last_sem,
):
    s = lax.axis_index("section")
    t = lax.axis_index("tensor")
    y = t // CORES
    c = t % CORES
    n_t = n_y * CORES
    chunk = img_hbm.shape[0]
    half = chunk // 2
    slots = img_hbm.shape[1]
    width = wk_hbm.shape[1]
    tokens, columns = q.shape
    heads = columns // HD
    group = columns // width
    far = [(ds, dy) for ds in range(1, n_s) for dy in range(1, n_y)]
    near_s = [(ds, 0) for ds in range(1, n_s)]
    near_y = [(0, dy) for dy in range(1, n_y)]

    def place(ds, dy):
        return ds * n_y + dy

    def to(ds, dy, other=False):
        core = 1 - c if other else c
        return {
            "section": lax.rem(s + ds, n_s),
            "tensor": lax.rem(y + dy, n_y) * CORES + core,
        }

    def rows_of(ds, dy, core):
        chip = lax.rem(s + ds + n_s, n_s) * n_t + lax.rem(y + dy + n_y, n_y) * CORES
        return pl.ds(pl.multiple_of((chip + core) * chunk, chunk), chunk)

    sent = []

    def send(src, dst, sem, device):
        copy = pltpu.make_async_remote_copy(
            src_ref=src, dst_ref=dst, send_sem=send_sem.at[len(sent)],
            recv_sem=sem, device_id=device, device_id_type=MESH,
        )
        copy.start()
        sent.append(copy)

    def arrive(dst, sem):
        pltpu.make_async_remote_copy(
            src_ref=dst, dst_ref=dst, send_sem=send_sem.at[0],
            recv_sem=sem, device_id=to(0, 0, True), device_id_type=MESH,
        ).wait_recv()

    local = []

    def bring(src, dst):
        copy = pltpu.make_async_copy(src, dst, local_sem.at[len(local)])
        copy.start()
        local.append(copy)
        return copy

    barrier = pltpu.get_barrier_semaphore()
    partners = [to(0, 0, True)] + [to(ds, dy) for ds, dy in near_s + near_y]
    for device in partners:
        pl.semaphore_signal(barrier, inc=1, device_id=device, device_id_type=MESH)
    own = bring(img_hbm, img.at[0, 0])
    parts = 4
    depth = w.shape[0] // parts
    weights = []
    for i in range(parts):
        piece = pl.ds(i * depth, depth)
        weights.append(bring(wk_hbm.at[piece], w.at[piece, pl.ds(0, width)]))
        weights.append(bring(wv_hbm.at[piece], w.at[piece, pl.ds(width, width)]))
    text = [bring(q_hbm, q), bring(cot_hbm, cot)]
    pl.semaphore_wait(barrier, len(partners))

    def piece_of(ds, dy, core, h):
        return img.at[place(ds, dy), core, pl.ds(h * half, half)]

    def own_piece(h):
        return img_hbm.at[pl.ds(h * half, half)]

    for h in range(2):
        for ds, dy in near_s:
            send(own_piece(h), piece_of(ds, dy, 0, h), img_sem.at[place(ds, dy), 0, h], to(ds, dy))
        for ds, dy in near_y:
            send(own_piece(1 - h), piece_of(ds, dy, 0, 1 - h), img_sem.at[place(ds, dy), 0, 1 - h], to(ds, dy))
    for h in range(2):
        send(own_piece(h), piece_of(0, 0, 1, h), img_sem.at[0, 1, h], to(0, 0, True))

    def receive(ds, dy, core, h):
        arrive(piece_of(ds, dy, core, h), img_sem.at[place(ds, dy), core, h])

    def share(ds, dy, h):
        send(piece_of(ds, dy, 0, h), piece_of(ds, dy, 1, h), img_sem.at[place(ds, dy), 1, h], to(0, 0, True))

    def project(ds, dy, core, first=0, length=chunk):
        start = rows_of(-ds, -dy, 1 - c if core else c).start + first
        features = img[place(ds, dy), core, pl.ds(first, length)]
        acc[...] += dot(features, w[pl.ds(pl.multiple_of(start, half), length), :], TN)

    def half_project(ds, dy, core, h):
        project(ds, dy, core, h * half, half)

    early = [(ds, dy, 0) for ds, dy in near_s] + [(ds, dy, 1) for ds, dy in near_y]
    late = [(ds, dy, 1) for ds, dy in near_s] + [(ds, dy, 0) for ds, dy in near_y]
    acc[...] = jnp.zeros_like(acc)
    own.wait()
    for copy in weights:
        copy.wait()
    project(0, 0, 0)
    for ds, dy in near_s:
        receive(ds, dy, 0, 0)
        for _, ey in near_y:
            send(piece_of(ds, 0, 0, 0), piece_of(ds, ey, 0, 0), img_sem.at[place(ds, ey), 0, 0], to(0, ey))
        share(ds, dy, 0)
    for ds, dy in near_y:
        receive(ds, dy, 0, 1)
        for es, _ in near_s:
            send(piece_of(0, dy, 0, 1), piece_of(es, dy, 0, 1), img_sem.at[place(es, dy), 0, 1], to(es, 0))
        share(ds, dy, 1)
    for h in range(2):
        receive(0, 0, 1, h)
    project(0, 0, 1)
    for copy in text:
        copy.wait()
    scale = jnp.tanh(jnp.full((1, HD), gates_ref[0], F32))
    for i in range(heads):
        part = pl.ds(i * HD, HD)
        cot[:, part] = (scale * cot[:, part].astype(F32)).astype(BF16)
    for unit in early:
        half_project(*unit[:2], 0, unit[2])
    for unit in early:
        receive(*unit[:2], 1, unit[2])
        half_project(*unit[:2], 1, unit[2])
    for unit in late:
        receive(*unit[:2], 0, unit[2])
        share(*unit)
    for unit in late:
        half_project(*unit[:2], 0, unit[2])
    for unit in late:
        receive(*unit[:2], 1, unit[2])
        half_project(*unit[:2], 1, unit[2])
    for ds, dy in far:
        receive(ds, dy, 0, 0)
        share(ds, dy, 0)
        half_project(ds, dy, 0, 0)
    for ds, dy in far:
        receive(ds, dy, 0, 1)
        share(ds, dy, 1)
    for ds, dy in far:
        half_project(ds, dy, 0, 1)
        receive(ds, dy, 1, 0)
        half_project(ds, dy, 1, 0)
    for ds, dy in far:
        receive(ds, dy, 1, 1)
        half_project(ds, dy, 1, 1)

    kv[...] = acc[...].astype(BF16)
    dk[...] = jnp.zeros_like(dk)
    dv[...] = jnp.zeros_like(dv)
    valid = tiles_ref[0] * TILE_TOK
    factor = 1.0 / math.sqrt(HD)

    def lanes(i, offset=0):
        return pl.ds(pl.multiple_of(i * HD + offset, HD), HD)

    def attend(b, carry):
        first = b * block
        j = first // group
        key = kv[:, lanes(j)]
        value = kv[:, lanes(j, width)]
        allowed = lax.broadcasted_iota(jnp.int32, (slots, tokens), 0) < valid
        total_k = dk[:, lanes(j)]
        total_v = dv[:, lanes(j)]
        for i in range(block):
            query = q[:, lanes(first + i)]
            upstream = cot[:, lanes(first + i)]
            scores = jnp.where(allowed, dot(key, query, NT) * factor, -1e30)
            expo = jnp.exp(scores - jnp.max(scores, axis=0, keepdims=True))
            probs = expo * (1.0 / jnp.sum(expo, axis=0, keepdims=True))
            probs_b = probs.astype(BF16)
            d_probs = dot(value, upstream, NT)
            delta = jnp.sum(probs * d_probs, axis=0, keepdims=True)
            d_scores = (probs * (d_probs - delta) * factor).astype(BF16)
            total_v += dot(probs_b, upstream, NN)
            total_k += dot(d_scores, query, NN)
            probs_t[first + i] = probs_b
            ds_t[first + i] = d_scores
        dk[:, lanes(j)] = total_k
        dv[:, lanes(j)] = total_v
        return carry

    lax.fori_loop(0, heads // block, attend, 0, unroll=True)
    dkv_t[:width, :] = dk[...].astype(BF16).T
    dkv_t[width:, :] = dv[...].astype(BF16).T

    def finish(b, carry):
        first = b * block
        j = first // group
        key = kv[:, lanes(j)]
        value = kv[:, lanes(j, width)]
        for i in range(block):
            context = dot(probs_t[first + i], value, TN)
            att[:, lanes(first + i)] = (scale * context).astype(BF16)
            dq[:, lanes(first + i)] = dot(ds_t[first + i], key, TN).astype(BF16)
        return carry

    def term(ds, dy, core):
        rows = rows_of(ds, dy, core)
        return dot(w[rows, :], dkv_t[...], NN)

    def start_pair(ds, dy):
        k = place(ds, dy)
        pair_out[k] = term(ds, dy, 1 - c).astype(BF16)
        send(pair_out.at[k], pair_in.at[k], pair_sem.at[k], to(0, 0, True))
        held[k] = term(ds, dy, c)

    def end_pair(ds, dy):
        k = place(ds, dy)
        arrive(pair_in.at[k], pair_sem.at[k])
        total = held[k] + pair_in[k].astype(F32)
        if (ds, dy) in far:
            out_send[k] = total.astype(BF16)
            send(out_send.at[k, pl.ds(0, half)], mid.at[0, k], mid_sem.at[0, k], to(ds, 0))
            send(out_send.at[k, pl.ds(half, half)], mid.at[1, k], mid_sem.at[1, k], to(0, dy))
        else:
            held[k] = total
            if (ds, dy) != (0, 0):
                h = 0 if ds else 1
                pass_on(ds, dy, h)

    def pass_on(ds, dy, h):
        k = place(ds, dy)
        piece = pl.ds(h * half, half)
        out_send[k, piece] = held[k, piece].astype(BF16)
        send(out_send.at[k, piece], last.at[k, piece], last_sem.at[k, h], to(ds, dy))

    order = far + near_s + near_y + [(0, 0)]
    for n, target in enumerate(order):
        start_pair(*target)
        if n:
            end_pair(*order[n - 1])
    end_pair(*order[-1])
    blocks = heads // block
    lax.fori_loop(0, blocks // 2, finish, 0)
    for ds, dy in near_s + near_y:
        k = place(ds, dy)
        h = 1 if ds else 0
        piece = pl.ds(h * half, half)
        for es, ey in far:
            if (es == ds) if ds else (ey == dy):
                m = place(es, ey)
                arrive(mid.at[h, m], mid_sem.at[h, m])
                held[k, piece] += mid[h, m].astype(F32)
        pass_on(ds, dy, h)
    lax.fori_loop(blocks // 2, blocks, finish, 0)
    total = held[0]
    for ds, dy in near_s + near_y:
        k = place(ds, dy)
        for h in range(2):
            arrive(last.at[k, pl.ds(h * half, half)], last_sem.at[k, h])
        total += last[k].astype(F32)
    dimg_ref[...] = total.astype(BF16)
    for copy in sent:
        copy.wait_send()


def write_out(count, *refs):
    sem = refs[-1]
    copies = [pltpu.make_async_copy(refs[i], refs[count + i], sem.at[i]) for i in range(count)]
    for copy in copies:
        copy.start()
    for copy in copies:
        copy.wait()


def solution(mesh):
    n_s = mesh.shape["section"]
    n_t = mesh.shape["tensor"]
    n_y = n_t // CORES
    chips = n_s * n_y

    def shards(queries, image, w_key, w_value, gates, tiles, cotangent):
        text, upstream = queries[0], cotangent[0]
        weight_key, weight_value = w_key[0], w_value[0]
        tokens, columns = text.shape
        d, width = weight_key.shape
        chunk, slots = image.shape
        heads = columns // HD
        group = columns // width
        block = math.gcd(group, 8)
        half = chunk // 2
        smem = pl.BlockSpec(memory_space=pltpu.SMEM)
        vmem = pl.BlockSpec(memory_space=pltpu.VMEM)
        hbm = pl.BlockSpec(memory_space=pltpu.HBM)
        dma = pltpu.SemaphoreType.DMA
        results = pl.pallas_call(
            functools.partial(kernel, n_s, n_y, block),
            out_shape=(
                pltpu.VMEM((tokens, columns), BF16),
                pltpu.VMEM((tokens, columns), BF16),
                pltpu.VMEM((chunk, slots), BF16),
            ),
            in_specs=[smem, smem] + [hbm] * 5,
            out_specs=(vmem, vmem, vmem),
            scratch_shapes=[
                pltpu.VMEM((d, 2 * width), BF16),
                pltpu.VMEM((tokens, columns), BF16),
                pltpu.VMEM((tokens, columns), BF16),
                pltpu.VMEM((chips, CORES, chunk, slots), BF16),
                pltpu.VMEM((slots, 2 * width), F32),
                pltpu.VMEM((slots, 2 * width), BF16),
                pltpu.VMEM((slots, width), F32),
                pltpu.VMEM((slots, width), F32),
                pltpu.VMEM((2 * width, slots), BF16),
                pltpu.VMEM((heads, slots, tokens), BF16),
                pltpu.VMEM((heads, slots, tokens), BF16),
                pltpu.VMEM((chips, chunk, slots), BF16),
                pltpu.VMEM((chips, chunk, slots), BF16),
                pltpu.VMEM((chips, chunk, slots), F32),
                pltpu.VMEM((chips, chunk, slots), BF16),
                pltpu.VMEM((2, chips, half, slots), BF16),
                pltpu.VMEM((chips, chunk, slots), BF16),
                dma((11,)),
                dma((counts(n_s, n_y),)),
                dma((chips, CORES, 2)),
                dma((chips,)),
                dma((2, chips)),
                dma((chips, 2)),
            ],
            compiler_params=pltpu.CompilerParams(
                collective_id=0, has_side_effects=True, vmem_limit_bytes=60 * 1024 * 1024
            ),
            cost_estimate=pl.CostEstimate(
                flops=8 * d * width * slots + 12 * tokens * columns * slots,
                bytes_accessed=4 * d * width + 8 * tokens * columns,
                transcendentals=heads * tokens * slots,
            ),
        )(gates, tiles, text, image, weight_key, weight_value, upstream)
        attended, d_query, d_image = pl.pallas_call(
            functools.partial(write_out, len(results)),
            out_shape=tuple(jax.ShapeDtypeStruct(a.shape, a.dtype) for a in results),
            in_specs=[vmem] * len(results),
            out_specs=tuple(hbm for _ in results),
            scratch_shapes=[dma((len(results),))],
            compiler_params=pltpu.CompilerParams(vmem_limit_bytes=8 * 1024 * 1024),
        )(*results)
        return attended[None], d_query[None], d_image

    return jax.shard_map(
        shards,
        mesh=mesh,
        in_specs=(
            P("section", "dp", "tensor"),
            P(("section", "tensor"), "dp"),
            P("section", None, "tensor"),
            P("section", None, "tensor"),
            P("section"),
            P("dp"),
            P("section", "dp", "tensor"),
        ),
        out_specs=(
            P("section", "dp", "tensor"),
            P("section", "dp", "tensor"),
            P(("section", "tensor"), "dp"),
        ),
        check_vma=False,
    )
```
